128 devices in a mesh: seg: 8 (over x_hi, z), seq: 16 (over x_lo, y, core).
Axes of the slice: x: 4 (x_hi: 2, x_lo: 2; x = x_hi * 2 + x_lo), y: 4, z: 4, core: 2. Of those that a mesh axis runs over, the one named last changes fastest.
Arguments:
- keyframe_latents: bfloat16 [8, 2048, 1536], P('seg', 'seq'), may hold values from -24 to 24
- keyframe_steps: int32 [8], P('seg'), may hold values from 0 to 63
- infill_latents: bfloat16 [8, 2, 2048, 1536], P('seg', None, 'seq'), may hold values from -24 to 24
- infill_steps: int32 [8, 2], P('seg'), may hold values from 0 to 63
- bounds: int32 [8, 2], P('seg'), may hold values from 0 to 7, as said below
- shift_table: float32 [64, 1536], replicated, may hold values from -4 to 4
- scale_table: float32 [64, 1536], replicated, may hold values from -0.5 to 1.5
- gate_table: float32 [64, 1536], replicated, may hold values from 0.5 to 2.5
- query_weight: bfloat16 [1536, 2048], P(None, 'seq'), may hold values from -0.15625 to 0.15625
- key_weight: bfloat16 [1536, 2048], P(None, 'seq'), may hold values from -0.15625 to 0.15625
- value_weight: bfloat16 [1536, 2048], P(None, 'seq'), may hold values from -0.15625 to 0.15625
- out_weight: bfloat16 [2048, 1536], P('seq'), may hold values from -0.125 to 0.125
- query_gain: float32 [128], replicated, may hold values from 0.5 to 2
- key_gain: float32 [128], replicated, may hold values from 0.5 to 2
Outputs:
- keyframe_out: bfloat16 [8, 2048, 1536], P('seg', 'seq')
- infill_out: bfloat16 [8, 2, 2048, 1536], P('seg', None, 'seq')
The draws below stay inside these ranges and needn't reach their ends.
Inputs may be any that keep to these rules, and one draw needn't show every extreme that they name: `bounds`: the two keyframes of a segment differ.
All inputs are finite; a program needn't handle non-finite values.
Results may differ from the reference program's by a relative error of at most 0.0052.
Values may be sent and summed in bfloat16 or wider, within the bound.
A program may use at most 192 MiB of HBM per device.

```python
import math
import jax
import jax.numpy as jnp
from jax import lax

D = 1536
HEADS = 16
HEAD = 128
STEPS = 64
FRAMES = 2
HD = 2048
FRAME_TOK = 2048
KEYS = 8
SEGS = 8


def latent_field(key, leading):
    key_feat, key_rows, key_base = jax.random.split(key, 3)
    features = jnp.exp(jax.random.uniform(key_feat, (D,), jnp.float32, math.log(0.3), math.log(3.0)))
    row_scales = jnp.exp(jax.random.uniform(key_rows, leading + (FRAME_TOK, 1), jnp.float32, math.log(0.5), math.log(2.0)))
    base = jax.random.normal(key_base, leading + (FRAME_TOK, D), jnp.float32)
    base = jnp.clip(base, -4.0, 4.0)
    return (base * features * row_scales).astype(jnp.bfloat16)


def draw_keyframe_latents(key, part):
    return latent_field(jax.random.fold_in(key, 11), (KEYS,))


def draw_infill_latents(key, part):
    return latent_field(jax.random.fold_in(key, 23), (SEGS, FRAMES))


def draw_bounds(key, part):
    key_left, key_step = jax.random.split(jax.random.fold_in(key, 37))
    left_one = jax.random.randint(key_left, (SEGS,), 0, KEYS, dtype=jnp.int32)
    stride = jax.random.randint(key_step, (SEGS,), 1, KEYS, dtype=jnp.int32)
    right_one = (left_one + stride) % KEYS
    return jnp.stack([left_one, right_one], axis=1).astype(jnp.int32)


def with_ends(entries, stream_key, smallest, top_value):
    spot = [jax.random.randint(jax.random.fold_in(stream_key, axis), (), 0, length) for axis, length in enumerate(entries.shape)]
    widest = entries.shape.index(max(entries.shape))
    neighbour = spot[:widest] + [(spot[widest] + 1) % entries.shape[widest]] + spot[widest + 1:]
    return entries.at[tuple(spot)].set(smallest).at[tuple(neighbour)].set(top_value)


def steps_of(rng, dims, cuts, least, largest):
    level, own = 1.0, jax.random.fold_in(rng, 6)
    for axis_at, parts in cuts:
        steps = jnp.exp(jax.random.uniform(jax.random.fold_in(own, axis_at), (parts,), jnp.float32, least / len(cuts), largest / len(cuts)))
        level = level * jnp.repeat(steps, dims[axis_at] // parts).reshape([-1 if axis == axis_at else 1 for axis in range(len(dims))])
    return level


def centred(key, extent, deviation, reach, cuts=(), kind=jnp.bfloat16):
    entries = deviation * jax.random.normal(key, extent, jnp.float32)
    if cuts:
        entries = entries * steps_of(key, extent, cuts, -0.22, 0.18)
    return jnp.clip(entries, -reach, reach).astype(kind)


def setup_inputs(seed: int = 0) -> dict:
    keys = jax.random.split(jax.random.key(seed), 15)
    return {
        "keyframe_latents": draw_keyframe_latents(jax.random.fold_in(keys[14], 71), 0),
        "keyframe_steps": with_ends(jax.random.randint(keys[1], (KEYS,), 0, STEPS), jax.random.fold_in(keys[1], 1), 0, STEPS - 1).astype(jnp.int32),
        "infill_latents": draw_infill_latents(jax.random.fold_in(keys[14], 71), 0),
        "infill_steps": with_ends(jax.random.randint(keys[3], (SEGS, FRAMES), 0, STEPS), jax.random.fold_in(keys[3], 1), 0, STEPS - 1).astype(jnp.int32),
        "bounds": draw_bounds(jax.random.fold_in(keys[14], 71), 0),
        "shift_table": centred(keys[5], (STEPS, D), 1.0, 4.0, (), jnp.float32),
        "scale_table": jnp.clip(jax.random.uniform(keys[6], (STEPS, D), jnp.float32, -0.5, 1.5), -0.5, 1.5),
        "gate_table": jnp.clip(jax.random.uniform(keys[7], (STEPS, D), jnp.float32, 0.5, 2.5), 0.5, 2.5),
        "query_weight": centred(keys[8], (D, HD), D ** -0.5, 0.15625, ((1, 16),)),
        "key_weight": centred(keys[9], (D, HD), D ** -0.5, 0.15625, ((1, 16),)),
        "value_weight": centred(keys[10], (D, HD), D ** -0.5, 0.15625, ((1, 16),)),
        "out_weight": centred(keys[11], (HD, D), HD ** -0.5, 0.125, ((0, 16),)),
        "query_gain": jnp.clip(jnp.exp(jax.random.uniform(keys[12], (HEAD,), jnp.float32, math.log(0.5), math.log(2.0))), 0.5, 2.0),
        "key_gain": jnp.clip(jnp.exp(jax.random.uniform(keys[13], (HEAD,), jnp.float32, math.log(0.5), math.log(2.0))), 0.5, 2.0),
    }


EPSILON = 1e-06

def lookup(steps, table):
    onehot = (steps[:, None] == jnp.arange(STEPS, dtype=jnp.int32)[None, :]).astype(jnp.float32)
    return jnp.dot(onehot, table, precision=lax.Precision.HIGHEST)

def modulate(latents, steps, shift_table, scale_table):
    shifts = lookup(steps, shift_table)
    scales = lookup(steps, scale_table)
    values = latents.astype(jnp.float32)
    center = values - lax.optimization_barrier(jnp.mean(values, axis=-1, keepdims=True))
    normed = center * lax.rsqrt(lax.optimization_barrier(jnp.mean(center * center, axis=-1, keepdims=True)) + EPSILON)
    return (normed * (1.0 + scales[:, None, :]) + shifts[:, None, :]).astype(jnp.bfloat16)

def head_norm(projected, gain):
    flat_rows = projected.shape[0]
    shaped = projected.reshape(flat_rows, HEADS, HEAD)
    normed = shaped * lax.rsqrt(lax.optimization_barrier(jnp.mean(shaped * shaped, axis=-1, keepdims=True)) + EPSILON) * gain
    return normed.reshape(flat_rows, HEADS * HEAD).astype(jnp.bfloat16)

def project(modded, query_weight, key_weight, value_weight, query_gain, key_gain):
    flat = modded.reshape(-1, D)
    query_rows = head_norm(jnp.dot(flat, query_weight, preferred_element_type=jnp.float32), query_gain)
    key_rows = head_norm(jnp.dot(flat, key_weight, preferred_element_type=jnp.float32), key_gain)
    value_rows = jnp.dot(flat, value_weight, preferred_element_type=jnp.float32).astype(jnp.bfloat16)
    shape = (modded.shape[0], FRAME_TOK, HEADS * HEAD)
    return (query_rows.reshape(shape), key_rows.reshape(shape), value_rows.reshape(shape))

def attend_head(query_rows, key_rows, value_rows):
    scores = jnp.dot(query_rows, key_rows.T, preferred_element_type=jnp.float32) * (1.0 / math.sqrt(HEAD))
    powers = jnp.exp(scores)
    weights = (powers / lax.optimization_barrier(jnp.sum(powers, axis=1, keepdims=True))).astype(jnp.bfloat16)
    return jnp.dot(weights, value_rows, preferred_element_type=jnp.float32).astype(jnp.bfloat16)

def split_heads(rows):
    return rows.reshape(rows.shape[0], HEADS, HEAD).transpose(1, 0, 2)

def attend_frame(query_rows, key_rows, value_rows):
    result = lax.map(lambda triple: attend_head(triple[0], triple[1], triple[2]), (split_heads(query_rows), split_heads(key_rows), split_heads(value_rows)))
    return result.transpose(1, 0, 2).reshape(query_rows.shape[0], HEADS * HEAD)

def finish(latents, steps, attention, out_weight, gate_table):
    gates = lookup(steps, gate_table)
    branch = jnp.dot(attention.reshape(-1, HEADS * HEAD), out_weight, preferred_element_type=jnp.float32)
    branch = branch.reshape(latents.shape)
    return (latents.astype(jnp.float32) + gates[:, None, :] * branch).astype(jnp.bfloat16)

def reference(keyframe_latents, keyframe_steps, infill_latents, infill_steps, bounds, shift_table, scale_table, gate_table, query_weight, key_weight, value_weight, out_weight, query_gain, key_gain):
    key_mod = modulate(keyframe_latents, keyframe_steps, shift_table, scale_table)
    key_query, key_keys, key_values = project(key_mod, query_weight, key_weight, value_weight, query_gain, key_gain)
    key_att = lax.map(lambda triple: attend_frame(triple[0], triple[1], triple[2]), (key_query, key_keys, key_values))
    keyframe_out = finish(keyframe_latents, keyframe_steps, key_att, out_weight, gate_table)
    flat_latents = infill_latents.reshape(SEGS * FRAMES, FRAME_TOK, D)
    flat_steps = infill_steps.reshape(SEGS * FRAMES)
    infill_mod = modulate(flat_latents, flat_steps, shift_table, scale_table)
    infill_query, infill_keys, infill_values = project(infill_mod, query_weight, key_weight, value_weight, query_gain, key_gain)
    owners = (jnp.arange(SEGS * FRAMES, dtype=jnp.int32) // FRAMES).astype(jnp.int32)
    left_index = bounds[owners, 0].astype(jnp.int32)
    right_index = bounds[owners, 1].astype(jnp.int32)

    def infill_frame(bundle):
        query_rows, own_keys, own_values, left_one, right_one = bundle
        key_rows = jnp.concatenate([own_keys, key_keys[left_one], key_keys[right_one]], axis=0)
        value_rows = jnp.concatenate([own_values, key_values[left_one], key_values[right_one]], axis=0)
        return attend_frame(query_rows, key_rows, value_rows)
    infill_att = lax.map(infill_frame, (infill_query, infill_keys, infill_values, left_index, right_index))
    infill_out = finish(flat_latents, flat_steps, infill_att, out_weight, gate_table)
    return (keyframe_out, infill_out.reshape(infill_latents.shape))
```

```python
import math

import jax
import jax.numpy as jnp
from jax import lax
from jax.experimental import pallas as pl
from jax.experimental.pallas import tpu as pltpu
from jax.sharding import PartitionSpec as P

MESH = pl.DeviceIdType.MESH
HEAD = 128
TOK = 128
SLOTS = 16
D = 1536
EPSILON = 1e-06
QSCALE = math.log2(math.e) / math.sqrt(HEAD)
OFFSETS = [(0, 0), (0, 3), (0, 1), (1, 0), (0, 2), (1, 3), (1, 1), (1, 2)]
POS = {o: i for i, o in enumerate(OFFSETS)}
CHUNKS = [(0, 2), (2, 8), (8, 12), (12, 16)]
PARTS = [(0, 8), (8, 12), (12, 16)]
QB = 512
KB = 512


def kernel(
    key_lat, inf_lat, key_steps, inf_steps, bounds, shift, scale, gate, wq, wk, wv, wo, qgain, kgain,
    key_out, inf_out,
    G, KV0, KV1, KV2, KO, Q, ACC, ATT, AR, W,
    g_send, g_recv, k_send, k_recv, a_send, a_recv,
):
    seg, seq = lax.axis_index("seg"), lax.axis_index("seq")
    xh, z = seg // 4, seg % 4
    xl, y, core = seq // 8, (seq // 2) % 4, seq % 2

    def at_seq(dx, dy, dc):
        x2 = 1 - xl if dx else xl
        c2 = 1 - core if dc else core
        return (seg, x2 * 8 + ((y + dy) % 4) * 2 + c2)

    def at_seg(dx, dz):
        x2 = 1 - xh if dx else xh
        return (x2 * 4 + (z + dz) % 4, seq)

    peers = [at_seq(*OFFSETS[r // 2], r % 2) for r in range(1, SLOTS)]
    peers += [at_seg(0, 1), at_seg(0, 3), at_seg(1, 0)]
    barrier = pltpu.get_barrier_semaphore()
    for peer in peers:
        pl.semaphore_signal(barrier, inc=1, device_id=peer, device_id_type=MESH)

    def g_copy(f, src, to, dst, sem, rows=None):
        a, b = G.at[f, src], G.at[f, dst]
        if rows is not None:
            a, b = G.at[f, src, pl.ds(*rows)], G.at[f, dst, pl.ds(*rows)]
        return pltpu.make_async_remote_copy(
            src_ref=a, dst_ref=b, send_sem=g_send.at[f], recv_sem=g_recv.at[f, sem],
            device_id=at_seq(*to), device_id_type=MESH,
        )

    LOW, HIGH = (0, TOK // 2), (TOK // 2, TOK // 2)
    S = {o: 2 * i for o, i in POS.items()}

    def send(f, src, to, dst, sem=None, rows=None):
        g_copy(f, src, to, dst, dst if sem is None else sem, rows).start()

    def took(f, slot, sem=None, rows=None):
        g_copy(f, slot, (0, 1, 0), slot, slot if sem is None else sem, rows).wait_recv()

    def sib(f, o):
        send(f, S[o], (0, 0, 1), S[o] + 1)

    def g_send_sib(f):
        sib(f, (0, 0))

    def g_send_y(f):
        send(f, 0, (0, 1, 0), S[0, 3])
        send(f, 0, (0, 3, 0), S[0, 1])

    def g_send_x(f):
        send(f, 0, (1, 0, 0), S[1, 0])

    def g_fwd_y(f):
        took(f, S[0, 3])
        send(f, S[0, 3], (0, 1, 0), S[0, 2], rows=LOW)
        sib(f, (0, 3))
        took(f, S[0, 1])
        send(f, S[0, 1], (0, 3, 0), S[0, 2], sem=16, rows=HIGH)
        sib(f, (0, 1))

    def g_fwd_x(f):
        took(f, S[1, 0])
        send(f, S[1, 0], (0, 1, 0), S[1, 3])
        send(f, S[1, 0], (0, 3, 0), S[1, 1])
        sib(f, (1, 0))

    def g_fwd_2(f):
        took(f, S[0, 2], rows=LOW)
        took(f, S[0, 2], sem=16, rows=HIGH)
        send(f, S[0, 2], (1, 0, 0), S[1, 2])
        sib(f, (0, 2))

    def g_fwd_3(f):
        took(f, S[1, 3])
        sib(f, (1, 3))
        took(f, S[1, 1])
        sib(f, (1, 1))

    def g_fwd_4(f):
        took(f, S[1, 2])
        sib(f, (1, 2))

    def g_sib(f, lo, hi):
        for r in range(lo, hi, 2):
            took(f, r + 1)

    KV = [KV0, KV1, KV2]

    def part_of(slot):
        n = [n for n, (lo, hi) in enumerate(PARTS) if lo <= slot < hi][0]
        return KV[n], PARTS[n][0]

    def k_copy(m, src, to, dst, sem, half=None):
        lo, hi = CHUNKS[m]
        part, base = part_of(lo)
        start, size = (lo - base) * TOK, (hi - lo) * TOK
        if half is not None:
            size //= 2
            start += half * size
        rows = pl.ds(start, size)
        return pltpu.make_async_remote_copy(
            src_ref=part.at[src, rows], dst_ref=part.at[dst, rows], send_sem=k_send.at[m], recv_sem=k_recv.at[m, sem],
            device_id=at_seg(*to), device_id_type=MESH,
        )

    def k_took(m, slot, sem=None, half=None):
        k_copy(m, slot, (0, 1), slot, slot if sem is None else sem, half).wait_recv()

    def k_send_0(m):
        k_copy(m, 0, (1, 0), POS[1, 0], POS[1, 0]).start()
        k_copy(m, 0, (0, 1), POS[0, 3], POS[0, 3]).start()
        k_copy(m, 0, (0, 3), POS[0, 1], POS[0, 1]).start()

    def k_fwd_1(m):
        k_took(m, POS[0, 3])
        k_copy(m, POS[0, 3], (0, 1), POS[0, 2], POS[0, 2], 0).start()
        k_took(m, POS[0, 1])
        k_copy(m, POS[0, 1], (0, 3), POS[0, 2], 8, 1).start()
        k_took(m, POS[1, 0])
        k_copy(m, POS[1, 0], (0, 1), POS[1, 3], POS[1, 3]).start()
        k_copy(m, POS[1, 0], (0, 3), POS[1, 1], POS[1, 1]).start()

    def k_fwd_2(m):
        k_took(m, POS[1, 3])
        k_copy(m, POS[1, 3], (0, 1), POS[1, 2], POS[1, 2], 0).start()
        k_took(m, POS[1, 1])
        k_copy(m, POS[1, 1], (0, 3), POS[1, 2], 9, 1).start()

    def k_done(m):
        k_took(m, POS[0, 2], half=0)
        k_took(m, POS[0, 2], sem=8, half=1)
        k_took(m, POS[1, 2], half=0)
        k_took(m, POS[1, 2], sem=9, half=1)

    def modulate(f):
        step = key_steps[0] if f == 0 else inf_steps[0, f - 1]
        gain = 1.0 + scale[pl.ds(step, 1), :]
        move = shift[pl.ds(step, 1), :]

        @pl.loop(0, TOK, step=32)
        def _(r):
            rows = pl.ds(r, 32)
            x = (key_lat[0, rows, :] if f == 0 else inf_lat[0, f - 1, rows, :]).astype(jnp.float32)
            x = x - jnp.mean(x, axis=-1, keepdims=True)
            x = x * lax.rsqrt(jnp.mean(x * x, axis=-1, keepdims=True) + EPSILON)
            G[f, 0, rows, :] = (x * gain + move).astype(jnp.bfloat16)

    qg = qgain[...].reshape(1, HEAD) * QSCALE
    kg = kgain[...].reshape(1, HEAD)

    def project(f, lo, hi):
        @pl.loop(lo // 2, hi // 2)
        def _(i):
            x = G[f, pl.ds(2 * i, 2)].reshape(2 * TOK, D)
            r = jnp.dot(x, W[...], preferred_element_type=jnp.float32)
            rows = pl.ds(pl.multiple_of(i * 2 * TOK, 2 * TOK), 2 * TOK)

            def norm(t, gain):
                return (t * lax.rsqrt(jnp.mean(t * t, axis=-1, keepdims=True) + EPSILON) * gain).astype(jnp.bfloat16)

            Q[f, rows, :] = norm(r[:, :HEAD], qg)
            kv = jnp.concatenate([norm(r[:, HEAD : 2 * HEAD], kg), r[:, 2 * HEAD :].astype(jnp.bfloat16)], axis=1)
            if f == 0:
                part, base = part_of(lo)
                part[0, pl.ds(pl.multiple_of((i - base // 2) * 2 * TOK, 2 * TOK), 2 * TOK), :] = kv
            else:
                KO[f - 1, rows, :] = kv

    ones = jnp.ones((KB, HEAD), jnp.bfloat16)

    def a_copy(f, r):
        o = OFFSETS[r // 2]
        back = 2 * POS[o[0], (4 - o[1]) % 4] + r % 2
        return pltpu.make_async_remote_copy(
            src_ref=ATT.at[f, r], dst_ref=AR.at[f, :, pl.ds(back * HEAD, HEAD)], send_sem=a_send.at[f],
            recv_sem=a_recv.at[f], device_id=at_seq(*o, r % 2), device_id_type=MESH,
        )

    def attend(f, lo, hi, sources, first, last, hooks=None):
        @pl.loop(lo, hi)
        def _(i):
            rows = pl.ds(pl.multiple_of(i * QB, QB), QB)
            q = Q[f, rows, :]
            a = None if first else ACC[f - 1, rows, :]
            for load in sources:
                kv = load()
                s = lax.dot_general(q, kv[:, :HEAD], (((1,), (1,)), ((), ())), preferred_element_type=jnp.float32)
                p = jnp.exp2(s).astype(jnp.bfloat16)
                v = jnp.concatenate([kv[:, HEAD:], ones], axis=1)
                t = jnp.dot(p, v, preferred_element_type=jnp.float32)
                a = t if a is None else a + t
            if not last:
                ACC[f - 1, rows, :] = a
            else:
                o = (a[:, :HEAD] / a[:, HEAD:]).astype(jnp.bfloat16)
                per = QB // TOK
                ATT[f, pl.ds(i * per, per)] = o.reshape(per, TOK, HEAD)
                for n in range(lo, hi):

                    @pl.when(i == n)
                    def _(n=n):
                        for r in range(n * per, (n + 1) * per):
                            if r == 0:
                                AR[f, :, 0:HEAD] = o[:TOK]
                            else:
                                a_copy(f, r).start()

            for n, hook in (hooks or {}).items():

                @pl.when(i == n)
                def _(hook=hook):
                    for h in hook:
                        h[0](*h[1:])

    def own(f):
        if f == 0:
            return [
                lambda n=n, j=j: KV[n][0, j * KB : (j + 1) * KB, :]
                for n, (lo, hi) in enumerate(PARTS)
                for j in range((hi - lo) * TOK // KB)
            ]
        return [lambda j=j: KO[f - 1, j * KB : (j + 1) * KB, :] for j in range(SLOTS * TOK // KB)]

    def slot_of(k):
        kx, kz = k // 4, k % 4
        dx = jnp.where(kx == xh, 0, 1)
        dz = (kz - z + 4) % 4
        slot = jnp.int32(0)
        for o, i in POS.items():
            slot = jnp.where((dx == o[0]) & (dz == o[1]), i, slot)
        return slot

    ends = [slot_of(bounds[0, 0]), slot_of(bounds[0, 1])]

    def cond(*parts):
        return [
            lambda n=n, t=t, j=j: KV[n][t, j * KB : (j + 1) * KB, :]
            for n in parts
            for j in range((PARTS[n][1] - PARTS[n][0]) * TOK // KB)
            for t in ends
        ]

    def finish():
        x = AR[...].reshape(3 * TOK, SLOTS * HEAD)

        @pl.loop(0, D // 256)
        def _(n):
            cols = pl.ds(pl.multiple_of(n * 256, 256), 256)
            w = G[3, :, :, cols].reshape(SLOTS * TOK, 256)
            t = jnp.dot(x, w, preferred_element_type=jnp.float32)
            for f in range(3):
                s = key_steps[0] if f == 0 else inf_steps[0, f - 1]
                g = gate[pl.ds(s, 1), cols]
                lat = (key_lat[0, :, cols] if f == 0 else inf_lat[0, f - 1, :, cols]).astype(jnp.float32)
                o = (lat + g * t[f * TOK : (f + 1) * TOK]).astype(jnp.bfloat16)
                if f == 0:
                    key_out[0, :, cols] = o
                else:
                    inf_out[0, f - 1, :, cols] = o

    modulate(0)
    pl.semaphore_wait(barrier, len(peers))
    g_send_sib(0)
    g_send_y(0)
    g_send_x(0)
    W[:, :HEAD] = wq[...]
    W[:, HEAD : 2 * HEAD] = wk[...]
    W[:, 2 * HEAD :] = wv[...]
    modulate(1)
    g_send_sib(1)
    g_sib(0, 0, 2)
    project(0, 0, 2)
    k_send_0(0)
    modulate(2)
    g_send_sib(2)
    G[3, 0] = wo[...]
    g_send_sib(3)

    g_fwd_y(0)
    g_fwd_x(0)
    g_send_x(1)
    k_fwd_1(0)
    g_sib(0, 2, 8)
    project(0, 2, 8)
    k_send_0(1)
    g_fwd_2(0)
    k_fwd_2(0)
    g_send_y(1)
    g_fwd_3(0)
    k_fwd_1(1)
    g_sib(0, 8, 12)
    project(0, 8, 12)
    k_send_0(2)
    g_fwd_4(0)
    g_sib(0, 12, 16)
    project(0, 12, 16)
    k_send_0(3)
    g_send_x(2)
    attend(0, 0, 4, own(0), True, True, {1: [(g_fwd_y, 1), (g_fwd_x, 1)], 2: [(k_fwd_2, 1)]})
    g_sib(1, 0, 8)
    project(1, 0, 8)
    g_fwd_2(1)
    g_send_y(2)
    k_fwd_1(2)
    k_done(0)
    k_done(1)
    attend(1, 0, 2, cond(0), True, False, {0: [(g_fwd_3, 1)]})
    g_fwd_4(1)
    g_send_x(3)
    k_fwd_2(2)
    g_sib(1, 8, 16)
    project(1, 8, 16)
    attend(1, 0, 2, own(1), False, False, {0: [(g_fwd_y, 2), (g_fwd_x, 2)]})
    k_fwd_1(3)
    attend(1, 2, 4, own(1), True, False, {2: [(g_fwd_2, 2)]})
    g_send_y(3)
    g_sib(2, 0, 8)
    project(2, 0, 8)
    k_done(2)
    attend(1, 2, 4, cond(0), False, False, {2: [(k_fwd_2, 3)]})
    attend(2, 0, 2, cond(0), True, False, {0: [(g_fwd_3, 2)]})
    g_fwd_4(2)
    g_sib(2, 8, 16)
    project(2, 8, 16)
    attend(2, 0, 2, own(2), False, False, {0: [(g_fwd_y, 3), (g_fwd_x, 3)]})
    attend(2, 2, 4, own(2), True, False, {2: [(g_fwd_2, 3)]})
    attend(2, 2, 4, cond(0), False, False)
    k_done(3)
    attend(1, 0, 4, cond(1, 2), False, True, {1: [(g_fwd_3, 3)], 3: [(g_fwd_4, 3)]})
    attend(2, 0, 4, cond(1, 2), False, True)
    g_sib(3, 0, 16)
    for f in range(3):
        whole = AR.at[f, :, pl.ds(HEAD, (SLOTS - 1) * HEAD)]
        pltpu.make_async_remote_copy(
            src_ref=whole, dst_ref=whole, send_sem=a_send.at[f], recv_sem=a_recv.at[f],
            device_id=at_seq(0, 1, 0), device_id_type=MESH,
        ).wait_recv()
    finish()

    for f in range(4):
        sent = G.at[f, pl.ds(0, 15)]
        pltpu.make_async_remote_copy(
            src_ref=sent, dst_ref=sent, send_sem=g_send.at[f], recv_sem=g_recv.at[f, 0],
            device_id=at_seq(0, 1, 0), device_id_type=MESH,
        ).wait_send()
    for m, (lo, hi) in enumerate(CHUNKS):
        part, base = part_of(lo)
        sent = part.at[pl.ds(0, 7), pl.ds((lo - base) * TOK, (hi - lo) * TOK)]
        pltpu.make_async_remote_copy(
            src_ref=sent, dst_ref=sent, send_sem=k_send.at[m], recv_sem=k_recv.at[m, 0],
            device_id=at_seg(0, 1), device_id_type=MESH,
        ).wait_send()
    for f in range(3):
        sent = ATT.at[f, pl.ds(1, 15)]
        pltpu.make_async_remote_copy(
            src_ref=sent, dst_ref=sent, send_sem=a_send.at[f], recv_sem=a_recv.at[f],
            device_id=at_seq(0, 1, 0), device_id_type=MESH,
        ).wait_send()


def local(
    keyframe_latents, keyframe_steps, infill_latents, infill_steps, bounds, shift_table, scale_table, gate_table,
    query_weight, key_weight, value_weight, out_weight, query_gain, key_gain,
):
    vmem, smem = pl.BlockSpec(memory_space=pltpu.VMEM), pl.BlockSpec(memory_space=pltpu.SMEM)
    bf16, f32 = jnp.bfloat16, jnp.float32
    n_tok = SLOTS * TOK
    return pl.pallas_call(
        kernel,
        name="diffusion_block",
        out_shape=(
            jax.ShapeDtypeStruct(keyframe_latents.shape, bf16),
            jax.ShapeDtypeStruct(infill_latents.shape, bf16),
        ),
        in_specs=[vmem, vmem, smem, smem, smem] + [vmem] * 9,
        out_specs=(vmem, vmem),
        scratch_shapes=[
            pltpu.VMEM((4, SLOTS, TOK, D), bf16),
            *[pltpu.VMEM((8, (hi - lo) * TOK, 2 * HEAD), bf16) for lo, hi in PARTS],
            pltpu.VMEM((2, n_tok, 2 * HEAD), bf16),
            pltpu.VMEM((3, n_tok, HEAD), bf16),
            pltpu.VMEM((2, n_tok, 2 * HEAD), f32),
            pltpu.VMEM((3, SLOTS, TOK, HEAD), bf16),
            pltpu.VMEM((3, TOK, SLOTS * HEAD), bf16),
            pltpu.VMEM((D, 3 * HEAD), bf16),
            pltpu.SemaphoreType.DMA((4,)),
            pltpu.SemaphoreType.DMA((4, 17)),
            pltpu.SemaphoreType.DMA((4,)),
            pltpu.SemaphoreType.DMA((4, 10)),
            pltpu.SemaphoreType.DMA((3,)),
            pltpu.SemaphoreType.DMA((3,)),
        ],
        compiler_params=pltpu.CompilerParams(
            collective_id=0, has_side_effects=True, vmem_limit_bytes=62 * 2**20
        ),
    )(
        keyframe_latents, infill_latents, keyframe_steps, infill_steps, bounds, shift_table, scale_table, gate_table,
        query_weight, key_weight, value_weight, out_weight, query_gain, key_gain,
    )


def solution(mesh):
    return jax.shard_map(
        local,
        mesh=mesh,
        in_specs=(
            P("seg", "seq", None), P("seg"), P("seg", None, "seq", None), P("seg", None), P("seg", None),
            P(), P(), P(), P(None, "seq"), P(None, "seq"), P(None, "seq"), P("seq", None), P(), P(),
        ),
        out_specs=(P("seg", "seq", None), P("seg", None, "seq", None)),
        check_vma=False,
    )
```

```python
import math

import jax
import jax.numpy as jnp
from jax import lax
from jax.experimental import pallas as pl
from jax.experimental.pallas import tpu as pltpu
from jax.sharding import PartitionSpec as P

MESH = pl.DeviceIdType.MESH
HEAD = 128
TOK = 128
SLOTS = 16
D = 1536
EPSILON = 1e-06
QSCALE = math.log2(math.e) / math.sqrt(HEAD)
OFFSETS = [(0, 0), (0, 3), (0, 1), (1, 0), (0, 2), (1, 3), (1, 1), (1, 2)]
POS = {o: i for i, o in enumerate(OFFSETS)}
ROUND_Y = (1, 2)
CHUNKS = [(0, 2), (2, 8), (8, 12), (12, 16)]
HALVES = [(0, 8), (8, 16)]
PARTS = [(0, 8), (8, 12), (12, 16)]
QB = 512
KB = 512

SCHEDULE = [
    "M0 gs0 gy0 gx0",
    "M1 gs1 M2 gs2",
    "P00 ks0 k1a0 k1b0",
    "fya0 fyb0 gx1 k1c0",
    "fx0 k2a0 k2b0 f20",
    "P01 kd0 ks1 gy1",
    "f3a0 f3b0 fx1 k1a1",
    "k1b1 P02 ks2 fya1",
    "fyb1 f40 k1c1 w0",
    "P10 k1a2 gy2 k1b2",
    "P03 ks3 A0o04 0@w1c",
    "1@f3a1 1@f3b1 1@k1c2 2@f21",
    "2@gx2 w1b k1c3 k2b1",
    "k2a1 k1a3 k1b3 f41",
    "w1a fx2 k2a2 k2b2",
    "fya2 w2 P11 A1o04",
    "0@w3 0@fyb2 P20 f3b2",
    "kd1 kd2 A2002 0@f22",
    "0@f3a2 0@k2a3 0@k2b3 A1004",
    "f42 kd3 A1104 P21",
    "A2024 2@w4a 2@w4b A2o04",
    "A2104 2@w5 wd",
]


def kernel(
    key_lat, inf_lat_hbm, key_steps, inf_steps, bounds, shift, scale, gate_hbm, wq, wk, wv, wo, qgain, kgain,
    key_out, inf_out,
    G, WG, KV0, KV1, KV2, KO, Q, ACC, ATT, AR, W, inf_lat, gate,
    g_send, g_recv, w_send, w_recv, k_send, k_recv, a_send, a_recv, loaded,
):
    seg, seq = lax.axis_index("seg"), lax.axis_index("seq")
    xh, z = seg // 4, seg % 4
    xl, y, core = seq // 8, (seq // 2) % 4, seq % 2

    def at_seq(dx, dy, dc):
        x2 = 1 - xl if dx else xl
        c2 = 1 - core if dc else core
        return (seg, x2 * 8 + ((y + dy) % 4) * 2 + c2)

    def at_seg(dx, dz):
        x2 = 1 - xh if dx else xh
        return (x2 * 4 + (z + dz) % 4, seq)

    peers = [at_seq(*OFFSETS[r // 2], r % 2) for r in range(1, SLOTS)]
    peers += [at_seg(0, 1), at_seg(0, 3), at_seg(1, 0)]
    barrier = pltpu.get_barrier_semaphore()
    for peer in peers:
        pl.semaphore_signal(barrier, inc=1, device_id=peer, device_id_type=MESH)

    loads = [
        pltpu.make_async_copy(wq, W.at[:, pl.ds(0, HEAD)], loaded.at[0]),
        pltpu.make_async_copy(wk, W.at[:, pl.ds(HEAD, HEAD)], loaded.at[1]),
        pltpu.make_async_copy(wv, W.at[:, pl.ds(2 * HEAD, HEAD)], loaded.at[2]),
        pltpu.make_async_copy(inf_lat_hbm, inf_lat, loaded.at[3]),
        pltpu.make_async_copy(wo, WG.at[0, 0], loaded.at[4]),
        pltpu.make_async_copy(gate_hbm, gate, loaded.at[5]),
    ]
    for load in loads:
        load.start()

    def g_copy(f, src, to, dst, sem, rows=None):
        a, b = G.at[f, src], G.at[f, dst]
        if rows is not None:
            a, b = G.at[f, src, pl.ds(*rows)], G.at[f, dst, pl.ds(*rows)]
        return pltpu.make_async_remote_copy(
            src_ref=a, dst_ref=b, send_sem=g_send.at[f], recv_sem=g_recv.at[f, sem],
            device_id=at_seq(*to), device_id_type=MESH,
        )

    LOW, HIGH = (0, TOK // 2), (TOK // 2, TOK // 2)
    S = {o: 2 * i for o, i in POS.items()}

    def send(f, src, to, dst, sem=None, rows=None):
        g_copy(f, src, to, dst, dst if sem is None else sem, rows).start()

    def took(f, slot, sem=None, rows=None):
        g_copy(f, slot, (0, 1, 0), slot, slot if sem is None else sem, rows).wait_recv()

    def sib(f, o):
        send(f, S[o], (0, 0, 1), S[o] + 1)

    def g_send_sib(f):
        sib(f, (0, 0))

    def g_send_y(f):
        send(f, 0, (0, 1, 0), S[0, 3])
        send(f, 0, (0, 3, 0), S[0, 1])

    def g_send_x(f):
        send(f, 0, (1, 0, 0), S[1, 0])

    def g_fwd_y(f):
        took(f, S[0, 3])
        send(f, S[0, 3], (0, 1, 0), S[0, 2], rows=LOW)
        sib(f, (0, 3))

    def g_fwd_y2(f):
        took(f, S[0, 1])
        send(f, S[0, 1], (0, 3, 0), S[0, 2], sem=16, rows=HIGH)
        sib(f, (0, 1))

    def g_fwd_x(f):
        took(f, S[1, 0])
        send(f, S[1, 0], (0, 1, 0), S[1, 3])
        send(f, S[1, 0], (0, 3, 0), S[1, 1])
        sib(f, (1, 0))

    def g_fwd_2(f):
        took(f, S[0, 2], rows=LOW)
        took(f, S[0, 2], sem=16, rows=HIGH)
        if f not in ROUND_Y:
            send(f, S[0, 2], (1, 0, 0), S[1, 2])
        sib(f, (0, 2))

    def g_fwd_3(f):
        took(f, S[1, 3])
        if f in ROUND_Y:
            send(f, S[1, 3], (0, 1, 0), S[1, 2], rows=LOW)
        sib(f, (1, 3))

    def g_fwd_32(f):
        took(f, S[1, 1])
        if f in ROUND_Y:
            send(f, S[1, 1], (0, 3, 0), S[1, 2], sem=17, rows=HIGH)
        sib(f, (1, 1))

    def g_fwd_4(f):
        if f in ROUND_Y:
            took(f, S[1, 2], rows=LOW)
            took(f, S[1, 2], sem=17, rows=HIGH)
        else:
            took(f, S[1, 2])
        sib(f, (1, 2))

    def g_sib(f, lo, hi):
        for r in range(lo, hi, 2):
            took(f, r + 1)

    def quarter(dz, part=0, parts=1):
        size = TOK // 4 // parts
        return pl.ds(pl.multiple_of(((z + dz) % 4) * (TOK // 4) + part * size, 16), size)

    def w_copy(src, dst, sem, to):
        return pltpu.make_async_remote_copy(
            src_ref=src, dst_ref=dst, send_sem=w_send, recv_sem=w_recv.at[sem], device_id=to, device_id_type=MESH
        )

    def w_seq(a, b, sem, to=(0, 1, 0), half=None):
        rows = quarter(0) if half is None else quarter(0, half, 2)
        return w_copy(WG.at[0, POS[a], rows], WG.at[0, POS[b], rows], sem, at_seq(*to))

    def w_seg(dz, sem, to=1, lo=1, hi=8):
        ref = WG.at[0, pl.ds(lo, hi - lo), quarter(dz)]
        return w_copy(ref, ref, sem, at_seg(0, to))

    def w_sib(dz):
        rows = quarter(dz)
        return w_copy(WG.at[0, pl.ds(1, 7), rows], WG.at[1, pl.ds(1, 7), rows], 13 + dz, at_seq(0, 0, 1))

    def w_sib_own():
        return w_copy(WG.at[0, 0], WG.at[1, 0], 12, at_seq(0, 0, 1))

    def w_0():
        need(4)
        w_sib_own().start()
        w_seq((0, 0), (0, 3), 0, (0, 1, 0)).start()
        w_seq((0, 0), (0, 1), 1, (0, 3, 0)).start()
        w_seq((0, 0), (1, 0), 2, (1, 0, 0)).start()

    def w_1():
        w_seq((0, 3), (0, 3), 0).wait_recv()
        w_seq((0, 3), (0, 2), 3, (0, 1, 0), 0).start()

    def w_1b():
        w_seq((0, 1), (0, 1), 1).wait_recv()
        w_seq((0, 1), (0, 2), 4, (0, 3, 0), 1).start()

    def w_1c():
        w_seq((1, 0), (1, 0), 2).wait_recv()
        w_seq((1, 0), (1, 3), 5, (0, 1, 0)).start()
        w_seq((1, 0), (1, 1), 6, (0, 3, 0)).start()

    def w_2():
        w_seq((0, 2), (0, 2), 3, half=0).wait_recv()
        w_seq((0, 2), (0, 2), 4, half=1).wait_recv()
        w_seq((0, 2), (1, 2), 7, (1, 0, 0)).start()

    def w_3():
        w_seq((1, 3), (1, 3), 5).wait_recv()
        w_seq((1, 1), (1, 1), 6).wait_recv()
        w_seq((1, 2), (1, 2), 7).wait_recv()
        w_seg(0, 8, 1).start()
        w_seg(0, 9, 3).start()
        w_sib(0).start()

    def w_4():
        w_seg(3, 8).wait_recv()
        w_seg(3, 10, 1, 1, 5).start()
        w_sib(3).start()

    def w_4b():
        w_seg(1, 9).wait_recv()
        w_seg(1, 11, 3, 5, 8).start()
        w_sib(1).start()

    def w_5():
        w_seg(2, 10, 1, 1, 5).wait_recv()
        w_seg(2, 11, 3, 5, 8).wait_recv()
        w_sib(2).start()

    def w_done():
        w_sib_own().wait_recv()
        for dz in range(4):
            w_sib(dz).wait_recv()

    KV = [KV0, KV1, KV2]

    def part_of(slot):
        n = [n for n, (lo, hi) in enumerate(PARTS) if lo <= slot < hi][0]
        return KV[n], PARTS[n][0]

    def k_copy(m, src, to, dst, sem, half=None):
        lo, hi = CHUNKS[m]
        part, base = part_of(lo)
        start, size = (lo - base) * TOK, (hi - lo) * TOK
        if half is not None:
            size //= 2
            start += half * size
        rows = pl.ds(start, size)
        return pltpu.make_async_remote_copy(
            src_ref=part.at[src, rows], dst_ref=part.at[dst, rows], send_sem=k_send.at[m], recv_sem=k_recv.at[m, sem],
            device_id=at_seg(*to), device_id_type=MESH,
        )

    def k_took(m, slot, sem=None, half=None):
        k_copy(m, slot, (0, 1), slot, slot if sem is None else sem, half).wait_recv()

    def k_send_0(m):
        k_copy(m, 0, (1, 0), POS[1, 0], POS[1, 0]).start()
        k_copy(m, 0, (0, 1), POS[0, 3], POS[0, 3]).start()
        k_copy(m, 0, (0, 3), POS[0, 1], POS[0, 1]).start()

    def k_fwd_1a(m):
        k_took(m, POS[0, 3])
        k_copy(m, POS[0, 3], (0, 1), POS[0, 2], POS[0, 2], 0).start()

    def k_fwd_1b(m):
        k_took(m, POS[0, 1])
        k_copy(m, POS[0, 1], (0, 3), POS[0, 2], 8, 1).start()

    def k_fwd_1c(m):
        k_took(m, POS[1, 0])
        k_copy(m, POS[1, 0], (0, 1), POS[1, 3], POS[1, 3]).start()
        k_copy(m, POS[1, 0], (0, 3), POS[1, 1], POS[1, 1]).start()

    def k_fwd_2a(m):
        k_took(m, POS[1, 3])
        k_copy(m, POS[1, 3], (0, 1), POS[1, 2], POS[1, 2], 0).start()

    def k_fwd_2b(m):
        k_took(m, POS[1, 1])
        k_copy(m, POS[1, 1], (0, 3), POS[1, 2], 9, 1).start()

    def k_done(m):
        k_took(m, POS[0, 2], half=0)
        k_took(m, POS[0, 2], sem=8, half=1)
        k_took(m, POS[1, 2], half=0)
        k_took(m, POS[1, 2], sem=9, half=1)

    def modulate(f):
        step = key_steps[0] if f == 0 else inf_steps[0, f - 1]
        gain = 1.0 + scale[pl.ds(step, 1), :]
        move = shift[pl.ds(step, 1), :]

        @pl.loop(0, TOK, step=32)
        def _(r):
            rows = pl.ds(r, 32)
            x = (key_lat[0, rows, :] if f == 0 else inf_lat[0, f - 1, rows, :]).astype(jnp.float32)
            x = x - jnp.mean(x, axis=-1, keepdims=True)
            x = x * lax.rsqrt(jnp.mean(x * x, axis=-1, keepdims=True) + EPSILON)
            G[f, 0, rows, :] = (x * gain + move).astype(jnp.bfloat16)

    qg = qgain[...].reshape(1, HEAD) * QSCALE
    kg = kgain[...].reshape(1, HEAD)

    def project(f, lo, hi):
        step = 4 if (hi - lo) % 4 == 0 else hi - lo
        size = step * TOK

        @pl.loop(0, (hi - lo) // step)
        def _(i):
            x = G[f, pl.ds(lo + step * i, step)].reshape(size, D)
            r = jnp.dot(x, W[...], preferred_element_type=jnp.float32)
            rows = pl.ds(pl.multiple_of(lo * TOK + i * size, 2 * TOK), size)

            def norm(t, gain):
                return (t * lax.rsqrt(jnp.mean(t * t, axis=-1, keepdims=True) + EPSILON) * gain).astype(jnp.bfloat16)

            Q[f, rows, :] = norm(r[:, :HEAD], qg)
            kv = jnp.concatenate([norm(r[:, HEAD : 2 * HEAD], kg), r[:, 2 * HEAD :].astype(jnp.bfloat16)], axis=1)
            if f == 0:
                part, base = part_of(lo)
                part[0, pl.ds(pl.multiple_of((lo - base) * TOK + i * size, 2 * TOK), size), :] = kv
            else:
                KO[f - 1, rows, :] = kv

    ones = jnp.ones((KB, HEAD), jnp.bfloat16)

    def a_copy(f, r):
        o = OFFSETS[r // 2]
        back = (r % 2) * (SLOTS // 2) + POS[o[0], (4 - o[1]) % 4]
        return pltpu.make_async_remote_copy(
            src_ref=ATT.at[f, r], dst_ref=AR.at[f, :, pl.ds(back * HEAD, HEAD)], send_sem=a_send.at[f],
            recv_sem=a_recv.at[f], device_id=at_seq(*o, r % 2), device_id_type=MESH,
        )

    def attend(f, lo, hi, sources, first, last, between):
        @pl.loop(lo, hi)
        def _(i):
            rows = pl.ds(pl.multiple_of(i * QB, QB), QB)
            q = Q[f, rows, :]
            a = None if first else ACC[f - 1, rows, :]
            for load in sources:
                kv = load()
                s = lax.dot_general(q, kv[:, :HEAD], (((1,), (1,)), ((), ())), preferred_element_type=jnp.float32)
                p = jnp.exp2(s).astype(jnp.bfloat16)
                v = jnp.concatenate([kv[:, HEAD:], ones], axis=1)
                t = jnp.dot(p, v, preferred_element_type=jnp.float32)
                a = t if a is None else a + t
            if not last:
                ACC[f - 1, rows, :] = a
            else:
                o = (a[:, :HEAD] / a[:, HEAD:]).astype(jnp.bfloat16)
                per = QB // TOK
                ATT[f, pl.ds(i * per, per)] = o.reshape(per, TOK, HEAD)
                for n in range(lo, hi):

                    @pl.when(i == n)
                    def _(n=n):
                        for r in range(n * per, (n + 1) * per):
                            if r == 0:
                                AR[f, :, 0:HEAD] = o[:TOK]
                            else:
                                a_copy(f, r).start()

            for n, then in between.items():
                pl.when(i == n)(then)

    def own(f):
        if f == 0:
            return [
                lambda n=n, j=j: KV[n][0, j * KB : (j + 1) * KB, :]
                for n, (lo, hi) in enumerate(PARTS)
                for j in range((hi - lo) * TOK // KB)
            ]
        return [lambda j=j: KO[f - 1, j * KB : (j + 1) * KB, :] for j in range(SLOTS * TOK // KB)]

    def slot_of(k):
        kx, kz = k // 4, k % 4
        dx = jnp.where(kx == xh, 0, 1)
        dz = (kz - z + 4) % 4
        slot = jnp.int32(0)
        for o, i in POS.items():
            slot = jnp.where((dx == o[0]) & (dz == o[1]), i, slot)
        return slot

    ends = [slot_of(bounds[0, 0]), slot_of(bounds[0, 1])]

    def cond(*parts):
        return [
            lambda n=n, t=t, j=j: KV[n][t, j * KB : (j + 1) * KB, :]
            for n in parts
            for j in range((PARTS[n][1] - PARTS[n][0]) * TOK // KB)
            for t in ends
        ]

    def finish():
        x = AR[...].reshape(3 * TOK, SLOTS * HEAD)

        @pl.loop(0, D // 256)
        def _(n):
            cols = pl.ds(pl.multiple_of(n * 256, 256), 256)
            w = WG[:, :, :, cols].reshape(SLOTS * TOK, 256)
            t = jnp.dot(x, w, preferred_element_type=jnp.float32)
            for f in range(3):
                s = key_steps[0] if f == 0 else inf_steps[0, f - 1]
                g = gate[pl.ds(s, 1), cols]
                lat = (key_lat[0, :, cols] if f == 0 else inf_lat[0, f - 1, :, cols]).astype(jnp.float32)
                o = (lat + g * t[f * TOK : (f + 1) * TOK]).astype(jnp.bfloat16)
                if f == 0:
                    key_out[0, :, cols] = o
                else:
                    inf_out[0, f - 1, :, cols] = o

    waited, begun = set(), set()

    def need(*which):
        for n in which:
            if n not in waited:
                waited.add(n)
                loads[n].wait()

    def do_modulate(f):
        if f:
            need(3)
        modulate(f)
        if f == 0:
            pl.semaphore_wait(barrier, len(peers))

    def do_project(f, n):
        need(0, 1, 2)
        lo, hi = (CHUNKS if f == 0 else HALVES)[n]
        g_sib(f, lo, hi)
        project(f, lo, hi)

    def do_attend(f, what, lo, hi, between):
        first = (f, lo) not in begun
        begun.update((f, i) for i in range(lo, hi))
        parts = {"o": own(f), "0": cond(0), "1": cond(1, 2)}[what]
        attend(f, lo, hi, parts, first, f == 0 or what == "1", between)

    simple = dict(
        gs=g_send_sib, gy=g_send_y, gx=g_send_x, fya=g_fwd_y, fyb=g_fwd_y2, fx=g_fwd_x, f2=g_fwd_2, f3a=g_fwd_3,
        f3b=g_fwd_32, f4=g_fwd_4, ks=k_send_0, k1a=k_fwd_1a, k1b=k_fwd_1b, k1c=k_fwd_1c, k2a=k_fwd_2a, k2b=k_fwd_2b,
        kd=k_done, M=do_modulate,
    )
    whole_w = dict(w0=w_0, w1a=w_1, w1b=w_1b, w1c=w_1c, w2=w_2, w3=w_3, w4a=w_4, w4b=w_4b, w5=w_5, wd=w_done)

    def run(op, between=()):
        if op in whole_w:
            whole_w[op]()
        elif op[0] == "P":
            do_project(int(op[1]), int(op[2]))
        elif op[0] == "A":
            steps = {n: [b[2:] for b in between if int(b[0]) == n] for n in {int(b[0]) for b in between}}
            thens = {n: lambda ops=ops: [run(o) for o in ops] and None for n, ops in steps.items()}
            do_attend(int(op[1]), op[2], int(op[3]), int(op[4]), thens)
        else:
            simple[op[:-1]](int(op[-1]))

    todo = [op for line in SCHEDULE for op in line.split()]
    while todo:
        op, inside = todo.pop(0), []
        while todo and todo[0][1] == "@":
            inside.append(todo.pop(0))
        run(op, inside)
    need(5)
    for f in range(3):
        whole = AR.at[f, :, pl.ds(HEAD, (SLOTS - 1) * HEAD)]
        pltpu.make_async_remote_copy(
            src_ref=whole, dst_ref=whole, send_sem=a_send.at[f], recv_sem=a_recv.at[f],
            device_id=at_seq(0, 1, 0), device_id_type=MESH,
        ).wait_recv()
    finish()

    for f in range(3):
        sent = G.at[f, pl.ds(0, 15)]
        pltpu.make_async_remote_copy(
            src_ref=sent, dst_ref=sent, send_sem=g_send.at[f], recv_sem=g_recv.at[f, 0],
            device_id=at_seq(0, 1, 0), device_id_type=MESH,
        ).wait_send()
    sent = G.at[0, pl.ds(0, 15)]
    w_copy(sent, sent, 0, at_seq(0, 1, 0)).wait_send()
    for m, (lo, hi) in enumerate(CHUNKS):
        part, base = part_of(lo)
        sent = part.at[pl.ds(0, 7), pl.ds((lo - base) * TOK, (hi - lo) * TOK)]
        pltpu.make_async_remote_copy(
            src_ref=sent, dst_ref=sent, send_sem=k_send.at[m], recv_sem=k_recv.at[m, 0],
            device_id=at_seg(0, 1), device_id_type=MESH,
        ).wait_send()
    for f in range(3):
        sent = ATT.at[f, pl.ds(1, 15)]
        pltpu.make_async_remote_copy(
            src_ref=sent, dst_ref=sent, send_sem=a_send.at[f], recv_sem=a_recv.at[f],
            device_id=at_seq(0, 1, 0), device_id_type=MESH,
        ).wait_send()


def local(
    keyframe_latents, keyframe_steps, infill_latents, infill_steps, bounds, shift_table, scale_table, gate_table,
    query_weight, key_weight, value_weight, out_weight, query_gain, key_gain,
):
    vmem, smem = pl.BlockSpec(memory_space=pltpu.VMEM), pl.BlockSpec(memory_space=pltpu.SMEM)
    hbm = pl.BlockSpec(memory_space=pl.ANY)
    bf16, f32 = jnp.bfloat16, jnp.float32
    n_tok = SLOTS * TOK
    return pl.pallas_call(
        kernel,
        name="diffusion_block",
        out_shape=(
            jax.ShapeDtypeStruct(keyframe_latents.shape, bf16),
            jax.ShapeDtypeStruct(infill_latents.shape, bf16),
        ),
        in_specs=[vmem, hbm, smem, smem, smem, vmem, vmem, hbm, hbm, hbm, hbm, hbm, vmem, vmem],
        out_specs=(vmem, vmem),
        scratch_shapes=[
            pltpu.VMEM((3, SLOTS, TOK, D), bf16),
            pltpu.VMEM((2, SLOTS // 2, TOK, D), bf16),
            *[pltpu.VMEM((8, (hi - lo) * TOK, 2 * HEAD), bf16) for lo, hi in PARTS],
            pltpu.VMEM((2, n_tok, 2 * HEAD), bf16),
            pltpu.VMEM((3, n_tok, HEAD), bf16),
            pltpu.VMEM((2, n_tok, 2 * HEAD), f32),
            pltpu.VMEM((3, SLOTS, TOK, HEAD), bf16),
            pltpu.VMEM((3, TOK, SLOTS * HEAD), bf16),
            pltpu.VMEM((D, 3 * HEAD), bf16),
            pltpu.VMEM(infill_latents.shape, bf16),
            pltpu.VMEM(gate_table.shape, f32),
            pltpu.SemaphoreType.DMA((3,)),
            pltpu.SemaphoreType.DMA((3, 18)),
            pltpu.SemaphoreType.DMA,
            pltpu.SemaphoreType.DMA((17,)),
            pltpu.SemaphoreType.DMA((4,)),
            pltpu.SemaphoreType.DMA((4, 10)),
            pltpu.SemaphoreType.DMA((3,)),
            pltpu.SemaphoreType.DMA((3,)),
            pltpu.SemaphoreType.DMA((6,)),
        ],
        compiler_params=pltpu.CompilerParams(
            collective_id=0, has_side_effects=True, vmem_limit_bytes=62 * 2**20
        ),
    )(
        keyframe_latents, infill_latents, keyframe_steps, infill_steps, bounds, shift_table, scale_table, gate_table,
        query_weight, key_weight, value_weight, out_weight, query_gain, key_gain,
    )


def solution(mesh):
    return jax.shard_map(
        local,
        mesh=mesh,
        in_specs=(
            P("seg", "seq", None), P("seg"), P("seg", None, "seq", None), P("seg", None), P("seg", None),
            P(), P(), P(), P(None, "seq"), P(None, "seq"), P(None, "seq"), P("seq", None), P(), P(),
        ),
        out_specs=(P("seg", "seq", None), P("seg", None, "seq", None)),
        check_vma=False,
    )
```

```python
import math

import jax
import jax.numpy as jnp
from jax import lax
from jax.experimental import pallas as pl
from jax.experimental.pallas import tpu as pltpu
from jax.sharding import PartitionSpec as P

MESH = pl.DeviceIdType.MESH
HEAD = 128
TOK = 128
SLOTS = 16
D = 1536
EPSILON = 1e-06
QSCALE = math.log2(math.e) / math.sqrt(HEAD)
OFFSETS = [(0, 0), (0, 3), (0, 1), (1, 0), (0, 2), (1, 3), (1, 1), (1, 2)]
POS = {o: i for i, o in enumerate(OFFSETS)}
ROUND_Y = (1, 2)
CHUNKS = [(0, 2), (2, 8), (8, 12), (12, 16)]
HALVES = [(0, 8), (8, 16)]
PARTS = [(0, 8), (8, 12), (12, 16)]
QB = 512
KB = 512

SCHEDULE = [
    "M0 gs0 gy0 gx0",
    "M1 gs1 M2 gs2",
    "P00 ks0 k1a0 k1b0",
    "fya0 fyb0 gx1 k1c0",
    "fx0 k2a0 k2b0 f20",
    "P01 kd0 gy1 ks1",
    "f3a0 f3b0 fx1 k1a1",
    "k1b1 P02 ks2 fya1",
    "fyb1 f40 k1c1 gx2",
    "P10 k1a2 gy2 k1b2",
    "w0 A1a02 f21 f3a1",
    "f3b1 P03 k1c2 ks3",
    "A0o04 2@w1a k2b1 k2a1",
    "f41 k2a2 fyb2 k2b2",
    "k1a3 k1b3 w1b w1c",
    "fx2 P11 fya2 A1b02",
    "A1b24 kd1 w2 k1c3",
    "A1a24 P20 kd2 w3",
    "A1104 A2102 0@f22 A2002",
    "f3a2 f3b2 k2a3 k2b3",
    "A2a02 A1004 2@f42 kd3",
    "A1224 A1202 P21 A2024",
    "2@w4a 2@w4b A2b02 A2202",
    "A2224 A2124 A2a24 A2b24",
    "2@w5 wd",
]


def kernel(
    key_lat, inf_lat_hbm, key_steps, inf_steps, bounds, shift, scale, gate_hbm, wq, wk, wv, wo, qgain, kgain,
    key_out, inf_out,
    G, WG, KV0, KV1, KV2, KO, Q, ACC, ATT, AR, W, inf_lat, gate,
    g_send, g_recv, w_send, w_recv, k_send, k_recv, a_send, a_recv, loaded,
):
    seg, seq = lax.axis_index("seg"), lax.axis_index("seq")
    xh, z = seg // 4, seg % 4
    xl, y, core = seq // 8, (seq // 2) % 4, seq % 2

    def at_seq(dx, dy, dc):
        x2 = 1 - xl if dx else xl
        c2 = 1 - core if dc else core
        return (seg, x2 * 8 + ((y + dy) % 4) * 2 + c2)

    def at_seg(dx, dz):
        x2 = 1 - xh if dx else xh
        return (x2 * 4 + (z + dz) % 4, seq)

    peers = [at_seq(*OFFSETS[r // 2], r % 2) for r in range(1, SLOTS)]
    peers += [at_seg(0, 1), at_seg(0, 3), at_seg(1, 0)]
    barrier = pltpu.get_barrier_semaphore()
    for peer in peers:
        pl.semaphore_signal(barrier, inc=1, device_id=peer, device_id_type=MESH)

    loads = [
        pltpu.make_async_copy(wq, W.at[:, pl.ds(0, HEAD)], loaded.at[0]),
        pltpu.make_async_copy(wk, W.at[:, pl.ds(HEAD, HEAD)], loaded.at[1]),
        pltpu.make_async_copy(wv, W.at[:, pl.ds(2 * HEAD, HEAD)], loaded.at[2]),
        pltpu.make_async_copy(inf_lat_hbm, inf_lat, loaded.at[3]),
        pltpu.make_async_copy(wo, WG.at[0, 0], loaded.at[4]),
        pltpu.make_async_copy(gate_hbm, gate, loaded.at[5]),
    ]
    for load in loads:
        load.start()

    def g_copy(f, src, to, dst, sem, rows=None):
        a, b = G.at[f, src], G.at[f, dst]
        if rows is not None:
            a, b = G.at[f, src, pl.ds(*rows)], G.at[f, dst, pl.ds(*rows)]
        return pltpu.make_async_remote_copy(
            src_ref=a, dst_ref=b, send_sem=g_send.at[f], recv_sem=g_recv.at[f, sem],
            device_id=at_seq(*to), device_id_type=MESH,
        )

    LOW, HIGH = (0, TOK // 2), (TOK // 2, TOK // 2)
    S = {o: 2 * i for o, i in POS.items()}

    def send(f, src, to, dst, sem=None, rows=None):
        g_copy(f, src, to, dst, dst if sem is None else sem, rows).start()

    def took(f, slot, sem=None, rows=None):
        g_copy(f, slot, (0, 1, 0), slot, slot if sem is None else sem, rows).wait_recv()

    def sib(f, o):
        send(f, S[o], (0, 0, 1), S[o] + 1)

    def g_send_sib(f):
        sib(f, (0, 0))

    def g_send_y(f):
        send(f, 0, (0, 1, 0), S[0, 3])
        send(f, 0, (0, 3, 0), S[0, 1])

    def g_send_x(f):
        send(f, 0, (1, 0, 0), S[1, 0])

    def g_fwd_y(f):
        took(f, S[0, 3])
        send(f, S[0, 3], (0, 1, 0), S[0, 2], rows=LOW)
        sib(f, (0, 3))

    def g_fwd_y2(f):
        took(f, S[0, 1])
        send(f, S[0, 1], (0, 3, 0), S[0, 2], sem=16, rows=HIGH)
        sib(f, (0, 1))

    def g_fwd_x(f):
        took(f, S[1, 0])
        send(f, S[1, 0], (0, 1, 0), S[1, 3])
        send(f, S[1, 0], (0, 3, 0), S[1, 1])
        sib(f, (1, 0))

    def g_fwd_2(f):
        took(f, S[0, 2], rows=LOW)
        took(f, S[0, 2], sem=16, rows=HIGH)
        if f not in ROUND_Y:
            send(f, S[0, 2], (1, 0, 0), S[1, 2])
        sib(f, (0, 2))

    def g_fwd_3(f):
        took(f, S[1, 3])
        if f in ROUND_Y:
            send(f, S[1, 3], (0, 1, 0), S[1, 2], rows=LOW)
        sib(f, (1, 3))

    def g_fwd_32(f):
        took(f, S[1, 1])
        if f in ROUND_Y:
            send(f, S[1, 1], (0, 3, 0), S[1, 2], sem=17, rows=HIGH)
        sib(f, (1, 1))

    def g_fwd_4(f):
        if f in ROUND_Y:
            took(f, S[1, 2], rows=LOW)
            took(f, S[1, 2], sem=17, rows=HIGH)
        else:
            took(f, S[1, 2])
        sib(f, (1, 2))

    def g_sib(f, lo, hi):
        for r in range(lo, hi, 2):
            took(f, r + 1)

    def quarter(dz, part=0, parts=1):
        size = TOK // 4 // parts
        return pl.ds(pl.multiple_of(((z + dz) % 4) * (TOK // 4) + part * size, 16), size)

    def w_copy(src, dst, sem, to):
        return pltpu.make_async_remote_copy(
            src_ref=src, dst_ref=dst, send_sem=w_send, recv_sem=w_recv.at[sem], device_id=to, device_id_type=MESH
        )

    def w_seq(a, b, sem, to=(0, 1, 0), half=None):
        rows = quarter(0) if half is None else quarter(0, half, 2)
        return w_copy(WG.at[0, POS[a], rows], WG.at[0, POS[b], rows], sem, at_seq(*to))

    def w_seg(dz, sem, to=1, lo=1, hi=8):
        ref = WG.at[0, pl.ds(lo, hi - lo), quarter(dz)]
        return w_copy(ref, ref, sem, at_seg(0, to))

    def w_sib(dz):
        rows = quarter(dz)
        return w_copy(WG.at[0, pl.ds(1, 7), rows], WG.at[1, pl.ds(1, 7), rows], 13 + dz, at_seq(0, 0, 1))

    def w_sib_own():
        return w_copy(WG.at[0, 0], WG.at[1, 0], 12, at_seq(0, 0, 1))

    def w_0():
        need(4)
        w_sib_own().start()
        w_seq((0, 0), (0, 3), 0, (0, 1, 0)).start()
        w_seq((0, 0), (0, 1), 1, (0, 3, 0)).start()
        w_seq((0, 0), (1, 0), 2, (1, 0, 0)).start()

    def w_1():
        w_seq((0, 3), (0, 3), 0).wait_recv()
        w_seq((0, 3), (0, 2), 3, (0, 1, 0), 0).start()

    def w_1b():
        w_seq((0, 1), (0, 1), 1).wait_recv()
        w_seq((0, 1), (0, 2), 4, (0, 3, 0), 1).start()

    def w_1c():
        w_seq((1, 0), (1, 0), 2).wait_recv()
        w_seq((1, 0), (1, 3), 5, (0, 1, 0)).start()
        w_seq((1, 0), (1, 1), 6, (0, 3, 0)).start()

    def w_2():
        w_seq((0, 2), (0, 2), 3, half=0).wait_recv()
        w_seq((0, 2), (0, 2), 4, half=1).wait_recv()
        w_seq((0, 2), (1, 2), 7, (1, 0, 0)).start()

    def w_3():
        w_seq((1, 3), (1, 3), 5).wait_recv()
        w_seq((1, 1), (1, 1), 6).wait_recv()
        w_seq((1, 2), (1, 2), 7).wait_recv()
        w_seg(0, 8, 1).start()
        w_seg(0, 9, 3).start()
        w_sib(0).start()

    def w_4():
        w_seg(3, 8).wait_recv()
        w_seg(3, 10, 1, 1, 5).start()
        w_sib(3).start()

    def w_4b():
        w_seg(1, 9).wait_recv()
        w_seg(1, 11, 3, 5, 8).start()
        w_sib(1).start()

    def w_5():
        w_seg(2, 10, 1, 1, 5).wait_recv()
        w_seg(2, 11, 3, 5, 8).wait_recv()
        w_sib(2).start()

    def w_done():
        w_sib_own().wait_recv()
        for dz in range(4):
            w_sib(dz).wait_recv()

    KV = [KV0, KV1, KV2]

    def part_of(slot):
        n = [n for n, (lo, hi) in enumerate(PARTS) if lo <= slot < hi][0]
        return KV[n], PARTS[n][0]

    def k_copy(m, src, to, dst, sem, half=None):
        lo, hi = CHUNKS[m]
        part, base = part_of(lo)
        start, size = (lo - base) * TOK, (hi - lo) * TOK
        if half is not None:
            size //= 2
            start += half * size
        rows = pl.ds(start, size)
        return pltpu.make_async_remote_copy(
            src_ref=part.at[src, rows], dst_ref=part.at[dst, rows], send_sem=k_send.at[m], recv_sem=k_recv.at[m, sem],
            device_id=at_seg(*to), device_id_type=MESH,
        )

    def k_took(m, slot, sem=None, half=None):
        k_copy(m, slot, (0, 1), slot, slot if sem is None else sem, half).wait_recv()

    def k_send_0(m):
        k_copy(m, 0, (1, 0), POS[1, 0], POS[1, 0]).start()
        k_copy(m, 0, (0, 1), POS[0, 3], POS[0, 3]).start()
        k_copy(m, 0, (0, 3), POS[0, 1], POS[0, 1]).start()

    def k_fwd_1a(m):
        k_took(m, POS[0, 3])
        k_copy(m, POS[0, 3], (0, 1), POS[0, 2], POS[0, 2], 0).start()

    def k_fwd_1b(m):
        k_took(m, POS[0, 1])
        k_copy(m, POS[0, 1], (0, 3), POS[0, 2], 8, 1).start()

    def k_fwd_1c(m):
        k_took(m, POS[1, 0])
        k_copy(m, POS[1, 0], (0, 1), POS[1, 3], POS[1, 3]).start()
        k_copy(m, POS[1, 0], (0, 3), POS[1, 1], POS[1, 1]).start()

    def k_fwd_2a(m):
        k_took(m, POS[1, 3])
        k_copy(m, POS[1, 3], (0, 1), POS[1, 2], POS[1, 2], 0).start()

    def k_fwd_2b(m):
        k_took(m, POS[1, 1])
        k_copy(m, POS[1, 1], (0, 3), POS[1, 2], 9, 1).start()

    def k_done(m):
        k_took(m, POS[0, 2], half=0)
        k_took(m, POS[0, 2], sem=8, half=1)
        k_took(m, POS[1, 2], half=0)
        k_took(m, POS[1, 2], sem=9, half=1)

    def modulate(f):
        step = key_steps[0] if f == 0 else inf_steps[0, f - 1]
        gain = 1.0 + scale[pl.ds(step, 1), :]
        move = shift[pl.ds(step, 1), :]

        @pl.loop(0, TOK, step=64)
        def _(r):
            rows = pl.ds(r, 64)
            x = (key_lat[0, rows, :] if f == 0 else inf_lat[0, f - 1, rows, :]).astype(jnp.float32)
            x = x - jnp.mean(x, axis=-1, keepdims=True)
            x = x * lax.rsqrt(jnp.mean(x * x, axis=-1, keepdims=True) + EPSILON)
            G[f, 0, rows, :] = (x * gain + move).astype(jnp.bfloat16)

    qg = qgain[...].reshape(1, HEAD) * QSCALE
    kg = kgain[...].reshape(1, HEAD)

    def project(f, lo, hi):
        step = 4 if (hi - lo) % 4 == 0 else hi - lo
        size = step * TOK

        @pl.loop(0, (hi - lo) // step)
        def _(i):
            x = G[f, pl.ds(lo + step * i, step)].reshape(size, D)
            r = jnp.dot(x, W[...], preferred_element_type=jnp.float32)
            rows = pl.ds(pl.multiple_of(lo * TOK + i * size, 2 * TOK), size)

            def norm(t, gain):
                return (t * lax.rsqrt(jnp.mean(t * t, axis=-1, keepdims=True) + EPSILON) * gain).astype(jnp.bfloat16)

            Q[f, rows, :] = norm(r[:, :HEAD], qg)
            kv = jnp.concatenate([norm(r[:, HEAD : 2 * HEAD], kg), r[:, 2 * HEAD :].astype(jnp.bfloat16)], axis=1)
            if f == 0:
                part, base = part_of(lo)
                part[0, pl.ds(pl.multiple_of((lo - base) * TOK + i * size, 2 * TOK), size), :] = kv
            else:
                KO[f - 1, rows, :] = kv

    ones = jnp.ones((KB, HEAD), jnp.bfloat16)

    def a_copy(f, r):
        o = OFFSETS[r // 2]
        back = (r % 2) * (SLOTS // 2) + POS[o[0], (4 - o[1]) % 4]
        return pltpu.make_async_remote_copy(
            src_ref=ATT.at[f, r], dst_ref=AR.at[f, :, pl.ds(back * HEAD, HEAD)], send_sem=a_send.at[f],
            recv_sem=a_recv.at[f], device_id=at_seq(*o, r % 2), device_id_type=MESH,
        )

    def attend(f, lo, hi, sources, first, last, between):
        @pl.loop(lo, hi)
        def _(i):
            rows = pl.ds(pl.multiple_of(i * QB, QB), QB)
            q = Q[f, rows, :]
            a = None if first else ACC[f - 1, rows, :]
            for load in sources:
                kv = load()
                s = lax.dot_general(q, kv[:, :HEAD], (((1,), (1,)), ((), ())), preferred_element_type=jnp.float32)
                p = jnp.exp2(s).astype(jnp.bfloat16)
                v = jnp.concatenate([kv[:, HEAD:], ones], axis=1)
                t = jnp.dot(p, v, preferred_element_type=jnp.float32)
                a = t if a is None else a + t
            if not last:
                ACC[f - 1, rows, :] = a
            else:
                o = (a[:, :HEAD] / a[:, HEAD:]).astype(jnp.bfloat16)
                per = QB // TOK
                ATT[f, pl.ds(i * per, per)] = o.reshape(per, TOK, HEAD)
                for n in range(lo, hi):

                    @pl.when(i == n)
                    def _(n=n):
                        for r in range(n * per, (n + 1) * per):
                            if r == 0:
                                AR[f, :, 0:HEAD] = o[:TOK]
                            else:
                                a_copy(f, r).start()

            for n, then in between.items():
                pl.when(i == n)(then)

    def own(f, part=0):
        if f == 0:
            return [
                lambda n=n, j=j: KV[n][0, j * KB : (j + 1) * KB, :]
                for n, (lo, hi) in enumerate(PARTS)
                for j in range((hi - lo) * TOK // KB)
            ]
        half = SLOTS * TOK // KB // 2
        return [
            lambda j=j: KO[f - 1, j * KB : (j + 1) * KB, :] for j in range(half * part, half * (part + 1))
        ]

    def slot_of(k):
        kx, kz = k // 4, k % 4
        dx = jnp.where(kx == xh, 0, 1)
        dz = (kz - z + 4) % 4
        slot = jnp.int32(0)
        for o, i in POS.items():
            slot = jnp.where((dx == o[0]) & (dz == o[1]), i, slot)
        return slot

    ends = [slot_of(bounds[0, 0]), slot_of(bounds[0, 1])]

    def cond(*parts):
        return [
            lambda n=n, t=t, j=j: KV[n][t, j * KB : (j + 1) * KB, :]
            for n in parts
            for j in range((PARTS[n][1] - PARTS[n][0]) * TOK // KB)
            for t in ends
        ]

    def finish():
        x = AR[...].reshape(3 * TOK, SLOTS * HEAD)

        @pl.loop(0, D // 768)
        def _(n):
            cols = pl.ds(pl.multiple_of(n * 768, 256), 768)
            w = WG[:, :, :, cols].reshape(SLOTS * TOK, 768)
            t = jnp.dot(x, w, preferred_element_type=jnp.float32)
            for f in range(3):
                s = key_steps[0] if f == 0 else inf_steps[0, f - 1]
                g = gate[pl.ds(s, 1), cols]
                lat = (key_lat[0, :, cols] if f == 0 else inf_lat[0, f - 1, :, cols]).astype(jnp.float32)
                o = (lat + g * t[f * TOK : (f + 1) * TOK]).astype(jnp.bfloat16)
                if f == 0:
                    key_out[0, :, cols] = o
                else:
                    inf_out[0, f - 1, :, cols] = o

    waited, begun = set(), {}

    def need(*which):
        for n in which:
            if n not in waited:
                waited.add(n)
                loads[n].wait()

    def do_modulate(f):
        if f:
            need(3)
        modulate(f)
        if f == 0:
            pl.semaphore_wait(barrier, len(peers))

    def do_project(f, n):
        need(0, 1, 2)
        lo, hi = (CHUNKS if f == 0 else HALVES)[n]
        g_sib(f, lo, hi)
        project(f, lo, hi)

    def do_attend(f, what, lo, hi, between):
        first = (f, lo) not in begun
        parts = {"o": (own, f), "a": (own, f, 0), "b": (own, f, 1), "0": (cond, 0), "1": (cond, 1), "2": (cond, 2)}[what]
        for i in range(lo, hi):
            begun[f, i] = begun.get((f, i), 0) + 1
        attend(f, lo, hi, parts[0](*parts[1:]), first, f == 0 or begun[f, lo] == 5, between)

    simple = dict(
        gs=g_send_sib, gy=g_send_y, gx=g_send_x, fya=g_fwd_y, fyb=g_fwd_y2, fx=g_fwd_x, f2=g_fwd_2, f3a=g_fwd_3,
        f3b=g_fwd_32, f4=g_fwd_4, ks=k_send_0, k1a=k_fwd_1a, k1b=k_fwd_1b, k1c=k_fwd_1c, k2a=k_fwd_2a, k2b=k_fwd_2b,
        kd=k_done, M=do_modulate,
    )
    whole_w = dict(w0=w_0, w1a=w_1, w1b=w_1b, w1c=w_1c, w2=w_2, w3=w_3, w4a=w_4, w4b=w_4b, w5=w_5, wd=w_done)

    def run(op, between=()):
        if op in whole_w:
            whole_w[op]()
        elif op[0] == "P":
            do_project(int(op[1]), int(op[2]))
        elif op[0] == "A":
            steps = {n: [b[2:] for b in between if int(b[0]) == n] for n in {int(b[0]) for b in between}}
            thens = {n: lambda ops=ops: [run(o) for o in ops] and None for n, ops in steps.items()}
            do_attend(int(op[1]), op[2], int(op[3]), int(op[4]), thens)
        else:
            simple[op[:-1]](int(op[-1]))

    todo = [op for line in SCHEDULE for op in line.split()]
    while todo:
        op, inside = todo.pop(0), []
        while todo and todo[0][1] == "@":
            inside.append(todo.pop(0))
        run(op, inside)
    need(5)
    for f in range(3):
        whole = AR.at[f, :, pl.ds(HEAD, (SLOTS - 1) * HEAD)]
        pltpu.make_async_remote_copy(
            src_ref=whole, dst_ref=whole, send_sem=a_send.at[f], recv_sem=a_recv.at[f],
            device_id=at_seq(0, 1, 0), device_id_type=MESH,
        ).wait_recv()
    finish()

    for f in range(3):
        sent = G.at[f, pl.ds(0, 15)]
        pltpu.make_async_remote_copy(
            src_ref=sent, dst_ref=sent, send_sem=g_send.at[f], recv_sem=g_recv.at[f, 0],
            device_id=at_seq(0, 1, 0), device_id_type=MESH,
        ).wait_send()
    sent = G.at[0, pl.ds(0, 15)]
    w_copy(sent, sent, 0, at_seq(0, 1, 0)).wait_send()
    for m, (lo, hi) in enumerate(CHUNKS):
        part, base = part_of(lo)
        sent = part.at[pl.ds(0, 7), pl.ds((lo - base) * TOK, (hi - lo) * TOK)]
        pltpu.make_async_remote_copy(
            src_ref=sent, dst_ref=sent, send_sem=k_send.at[m], recv_sem=k_recv.at[m, 0],
            device_id=at_seg(0, 1), device_id_type=MESH,
        ).wait_send()
    for f in range(3):
        sent = ATT.at[f, pl.ds(1, 15)]
        pltpu.make_async_remote_copy(
            src_ref=sent, dst_ref=sent, send_sem=a_send.at[f], recv_sem=a_recv.at[f],
            device_id=at_seq(0, 1, 0), device_id_type=MESH,
        ).wait_send()


def local(
    keyframe_latents, keyframe_steps, infill_latents, infill_steps, bounds, shift_table, scale_table, gate_table,
    query_weight, key_weight, value_weight, out_weight, query_gain, key_gain,
):
    vmem, smem = pl.BlockSpec(memory_space=pltpu.VMEM), pl.BlockSpec(memory_space=pltpu.SMEM)
    hbm = pl.BlockSpec(memory_space=pl.ANY)
    bf16, f32 = jnp.bfloat16, jnp.float32
    n_tok = SLOTS * TOK
    return pl.pallas_call(
        kernel,
        name="diffusion_block",
        out_shape=(
            jax.ShapeDtypeStruct(keyframe_latents.shape, bf16),
            jax.ShapeDtypeStruct(infill_latents.shape, bf16),
        ),
        in_specs=[vmem, hbm, smem, smem, smem, vmem, vmem, hbm, hbm, hbm, hbm, hbm, vmem, vmem],
        out_specs=(vmem, vmem),
        scratch_shapes=[
            pltpu.VMEM((3, SLOTS, TOK, D), bf16),
            pltpu.VMEM((2, SLOTS // 2, TOK, D), bf16),
            *[pltpu.VMEM((8, (hi - lo) * TOK, 2 * HEAD), bf16) for lo, hi in PARTS],
            pltpu.VMEM((2, n_tok, 2 * HEAD), bf16),
            pltpu.VMEM((3, n_tok, HEAD), bf16),
            pltpu.VMEM((2, n_tok, 2 * HEAD), f32),
            pltpu.VMEM((3, SLOTS, TOK, HEAD), bf16),
            pltpu.VMEM((3, TOK, SLOTS * HEAD), bf16),
            pltpu.VMEM((D, 3 * HEAD), bf16),
            pltpu.VMEM(infill_latents.shape, bf16),
            pltpu.VMEM(gate_table.shape, f32),
            pltpu.SemaphoreType.DMA((3,)),
            pltpu.SemaphoreType.DMA((3, 18)),
            pltpu.SemaphoreType.DMA,
            pltpu.SemaphoreType.DMA((17,)),
            pltpu.SemaphoreType.DMA((4,)),
            pltpu.SemaphoreType.DMA((4, 10)),
            pltpu.SemaphoreType.DMA((3,)),
            pltpu.SemaphoreType.DMA((3,)),
            pltpu.SemaphoreType.DMA((6,)),
        ],
        compiler_params=pltpu.CompilerParams(
            collective_id=0, has_side_effects=True, vmem_limit_bytes=62 * 2**20
        ),
    )(
        keyframe_latents, infill_latents, keyframe_steps, infill_steps, bounds, shift_table, scale_table, gate_table,
        query_weight, key_weight, value_weight, out_weight, query_gain, key_gain,
    )


def solution(mesh):
    return jax.shard_map(
        local,
        mesh=mesh,
        in_specs=(
            P("seg", "seq", None), P("seg"), P("seg", None, "seq", None), P("seg", None), P("seg", None),
            P(), P(), P(), P(None, "seq"), P(None, "seq"), P(None, "seq"), P("seq", None), P(), P(),
        ),
        out_specs=(P("seg", "seq", None), P("seg", None, "seq", None)),
        check_vma=False,
    )
```

```python
import math

import jax
import jax.numpy as jnp
from jax import lax
from jax.experimental import pallas as pl
from jax.experimental.pallas import tpu as pltpu
from jax.sharding import PartitionSpec as P

MESH = pl.DeviceIdType.MESH
HEAD = 128
TOK = 128
SLOTS = 16
D = 1536
EPSILON = 1e-06
QSCALE = math.log2(math.e) / math.sqrt(HEAD)
OFFSETS = [(0, 0), (0, 3), (0, 1), (1, 0), (0, 2), (1, 3), (1, 1), (1, 2)]
POS = {o: i for i, o in enumerate(OFFSETS)}
ROUND_Y = (1, 2)
CHUNKS = [(0, 2), (2, 8), (8, 12), (12, 16)]
HALVES = [(0, 8), (8, 16)]
PARTS = [(0, 8), (8, 12), (12, 16)]
QB = 512
KB = 256

SCHEDULE = [
    "M0 gs0 gy0 gx0",
    "M1 gs1 M2 gs2",
    "P00 ks0 k1a0 k1b0",
    "fya0 fyb0 gx1 k1c0",
    "fx0 k2a0 k2b0 f20",
    "P01 kd0 gy1 ks1",
    "f3a0 f3b0 fx1 k1a1",
    "k1b1 P02 ks2 fya1",
    "fyb1 f40 k1c1 gx2",
    "P10 k1a2 gy2 k1b2",
    "w0 A1a02 f21 f3a1",
    "f3b1 P03 k1c2 ks3",
    "A0o04 2@w1a k2b1 k2a1",
    "f41 k2a2 fyb2 k2b2",
    "k1a3 k1b3 w1b w1c",
    "fx2 P11 fya2 A1b02",
    "A1b24 kd1 w2 k1c3",
    "A1a24 P20 kd2 w3",
    "A1104 A2102 0@f22 A2002",
    "f3a2 f3b2 k2a3 k2b3",
    "A2a02 A1004 2@f42 kd3",
    "A1224 A1202 P21 A2024",
    "2@w4a 2@w4b A2b02 A2202",
    "A2224 A2124 A2a24 A2b24",
    "2@w5 wd",
]


def kernel(
    key_lat, inf_lat_hbm, key_steps, inf_steps, bounds, shift, scale, gate_hbm, wq, wk, wv, wo, qgain, kgain,
    key_out, inf_out,
    G, WG, KV0, KV1, KV2, KO, Q, ACC, ATT, AR, W, inf_lat, gate,
    g_send, g_recv, w_send, w_recv, k_send, k_recv, a_send, a_recv, loaded,
):
    seg, seq = lax.axis_index("seg"), lax.axis_index("seq")
    xh, z = seg // 4, seg % 4
    xl, y, core = seq // 8, (seq // 2) % 4, seq % 2

    def at_seq(dx, dy, dc):
        x2 = 1 - xl if dx else xl
        c2 = 1 - core if dc else core
        return (seg, x2 * 8 + ((y + dy) % 4) * 2 + c2)

    def at_seg(dx, dz):
        x2 = 1 - xh if dx else xh
        return (x2 * 4 + (z + dz) % 4, seq)

    peers = [at_seq(*OFFSETS[r // 2], r % 2) for r in range(1, SLOTS)]
    peers += [at_seg(0, 1), at_seg(0, 3), at_seg(1, 0)]
    barrier = pltpu.get_barrier_semaphore()
    for peer in peers:
        pl.semaphore_signal(barrier, inc=1, device_id=peer, device_id_type=MESH)

    loads = [
        pltpu.make_async_copy(wq, W.at[:, pl.ds(0, HEAD)], loaded.at[0]),
        pltpu.make_async_copy(wk, W.at[:, pl.ds(HEAD, HEAD)], loaded.at[1]),
        pltpu.make_async_copy(wv, W.at[:, pl.ds(2 * HEAD, HEAD)], loaded.at[2]),
        pltpu.make_async_copy(inf_lat_hbm, inf_lat, loaded.at[3]),
        pltpu.make_async_copy(wo, WG.at[0, 0], loaded.at[4]),
        pltpu.make_async_copy(gate_hbm, gate, loaded.at[5]),
    ]
    for load in loads:
        load.start()

    def g_copy(f, src, to, dst, sem, rows=None):
        a, b = G.at[f, src], G.at[f, dst]
        if rows is not None:
            a, b = G.at[f, src, pl.ds(*rows)], G.at[f, dst, pl.ds(*rows)]
        return pltpu.make_async_remote_copy(
            src_ref=a, dst_ref=b, send_sem=g_send.at[f], recv_sem=g_recv.at[f, sem],
            device_id=at_seq(*to), device_id_type=MESH,
        )

    LOW, HIGH = (0, TOK // 2), (TOK // 2, TOK // 2)
    S = {o: 2 * i for o, i in POS.items()}

    def send(f, src, to, dst, sem=None, rows=None):
        g_copy(f, src, to, dst, dst if sem is None else sem, rows).start()

    def took(f, slot, sem=None, rows=None):
        g_copy(f, slot, (0, 1, 0), slot, slot if sem is None else sem, rows).wait_recv()

    def sib(f, o):
        send(f, S[o], (0, 0, 1), S[o] + 1)

    def g_send_sib(f):
        sib(f, (0, 0))

    def g_send_y(f):
        send(f, 0, (0, 1, 0), S[0, 3])
        send(f, 0, (0, 3, 0), S[0, 1])

    def g_send_x(f):
        send(f, 0, (1, 0, 0), S[1, 0])

    def g_fwd_y(f):
        took(f, S[0, 3])
        send(f, S[0, 3], (0, 1, 0), S[0, 2], rows=LOW)
        sib(f, (0, 3))

    def g_fwd_y2(f):
        took(f, S[0, 1])
        send(f, S[0, 1], (0, 3, 0), S[0, 2], sem=16, rows=HIGH)
        sib(f, (0, 1))

    def g_fwd_x(f):
        took(f, S[1, 0])
        send(f, S[1, 0], (0, 1, 0), S[1, 3])
        send(f, S[1, 0], (0, 3, 0), S[1, 1])
        sib(f, (1, 0))

    def g_fwd_2(f):
        took(f, S[0, 2], rows=LOW)
        took(f, S[0, 2], sem=16, rows=HIGH)
        if f not in ROUND_Y:
            send(f, S[0, 2], (1, 0, 0), S[1, 2])
        sib(f, (0, 2))

    def g_fwd_3(f):
        took(f, S[1, 3])
        if f in ROUND_Y:
            send(f, S[1, 3], (0, 1, 0), S[1, 2], rows=LOW)
        sib(f, (1, 3))

    def g_fwd_32(f):
        took(f, S[1, 1])
        if f in ROUND_Y:
            send(f, S[1, 1], (0, 3, 0), S[1, 2], sem=17, rows=HIGH)
        sib(f, (1, 1))

    def g_fwd_4(f):
        if f in ROUND_Y:
            took(f, S[1, 2], rows=LOW)
            took(f, S[1, 2], sem=17, rows=HIGH)
        else:
            took(f, S[1, 2])
        sib(f, (1, 2))

    def g_sib(f, lo, hi):
        for r in range(lo, hi, 2):
            took(f, r + 1)

    def quarter(dz, part=0, parts=1):
        size = TOK // 4 // parts
        return pl.ds(pl.multiple_of(((z + dz) % 4) * (TOK // 4) + part * size, 16), size)

    def w_copy(src, dst, sem, to):
        return pltpu.make_async_remote_copy(
            src_ref=src, dst_ref=dst, send_sem=w_send, recv_sem=w_recv.at[sem], device_id=to, device_id_type=MESH
        )

    def w_seq(a, b, sem, to=(0, 1, 0), half=None):
        rows = quarter(0) if half is None else quarter(0, half, 2)
        return w_copy(WG.at[0, POS[a], rows], WG.at[0, POS[b], rows], sem, at_seq(*to))

    def w_seg(dz, sem, to=1, lo=1, hi=8):
        ref = WG.at[0, pl.ds(lo, hi - lo), quarter(dz)]
        return w_copy(ref, ref, sem, at_seg(0, to))

    def w_sib(dz):
        rows = quarter(dz)
        return w_copy(WG.at[0, pl.ds(1, 7), rows], WG.at[1, pl.ds(1, 7), rows], 13 + dz, at_seq(0, 0, 1))

    def w_sib_own():
        return w_copy(WG.at[0, 0], WG.at[1, 0], 12, at_seq(0, 0, 1))

    def w_0():
        need(4)
        w_sib_own().start()
        w_seq((0, 0), (0, 3), 0, (0, 1, 0)).start()
        w_seq((0, 0), (0, 1), 1, (0, 3, 0)).start()
        w_seq((0, 0), (1, 0), 2, (1, 0, 0)).start()

    def w_1():
        w_seq((0, 3), (0, 3), 0).wait_recv()
        w_seq((0, 3), (0, 2), 3, (0, 1, 0), 0).start()

    def w_1b():
        w_seq((0, 1), (0, 1), 1).wait_recv()
        w_seq((0, 1), (0, 2), 4, (0, 3, 0), 1).start()

    def w_1c():
        w_seq((1, 0), (1, 0), 2).wait_recv()
        w_seq((1, 0), (1, 3), 5, (0, 1, 0)).start()
        w_seq((1, 0), (1, 1), 6, (0, 3, 0)).start()

    def w_2():
        w_seq((0, 2), (0, 2), 3, half=0).wait_recv()
        w_seq((0, 2), (0, 2), 4, half=1).wait_recv()
        w_seq((0, 2), (1, 2), 7, (1, 0, 0)).start()

    def w_3():
        w_seq((1, 3), (1, 3), 5).wait_recv()
        w_seq((1, 1), (1, 1), 6).wait_recv()
        w_seq((1, 2), (1, 2), 7).wait_recv()
        w_seg(0, 8, 1).start()
        w_seg(0, 9, 3).start()
        w_sib(0).start()

    def w_4():
        w_seg(3, 8).wait_recv()
        w_seg(3, 10, 1, 1, 5).start()
        w_sib(3).start()

    def w_4b():
        w_seg(1, 9).wait_recv()
        w_seg(1, 11, 3, 5, 8).start()
        w_sib(1).start()

    def w_5():
        w_seg(2, 10, 1, 1, 5).wait_recv()
        w_seg(2, 11, 3, 5, 8).wait_recv()
        w_sib(2).start()

    def w_done():
        w_sib_own().wait_recv()
        for dz in range(4):
            w_sib(dz).wait_recv()

    KV = [KV0, KV1, KV2]

    def part_of(slot):
        n = [n for n, (lo, hi) in enumerate(PARTS) if lo <= slot < hi][0]
        return KV[n], PARTS[n][0]

    def k_copy(m, src, to, dst, sem, half=None):
        lo, hi = CHUNKS[m]
        part, base = part_of(lo)
        start, size = (lo - base) * TOK, (hi - lo) * TOK
        if half is not None:
            size //= 2
            start += half * size
        rows = pl.ds(start, size)
        return pltpu.make_async_remote_copy(
            src_ref=part.at[src, rows], dst_ref=part.at[dst, rows], send_sem=k_send.at[m], recv_sem=k_recv.at[m, sem],
            device_id=at_seg(*to), device_id_type=MESH,
        )

    def k_took(m, slot, sem=None, half=None):
        k_copy(m, slot, (0, 1), slot, slot if sem is None else sem, half).wait_recv()

    def k_send_0(m):
        k_copy(m, 0, (1, 0), POS[1, 0], POS[1, 0]).start()
        k_copy(m, 0, (0, 1), POS[0, 3], POS[0, 3]).start()
        k_copy(m, 0, (0, 3), POS[0, 1], POS[0, 1]).start()

    def k_fwd_1a(m):
        k_took(m, POS[0, 3])
        k_copy(m, POS[0, 3], (0, 1), POS[0, 2], POS[0, 2], 0).start()

    def k_fwd_1b(m):
        k_took(m, POS[0, 1])
        k_copy(m, POS[0, 1], (0, 3), POS[0, 2], 8, 1).start()

    def k_fwd_1c(m):
        k_took(m, POS[1, 0])
        k_copy(m, POS[1, 0], (0, 1), POS[1, 3], POS[1, 3]).start()
        k_copy(m, POS[1, 0], (0, 3), POS[1, 1], POS[1, 1]).start()

    def k_fwd_2a(m):
        k_took(m, POS[1, 3])
        k_copy(m, POS[1, 3], (0, 1), POS[1, 2], POS[1, 2], 0).start()

    def k_fwd_2b(m):
        k_took(m, POS[1, 1])
        k_copy(m, POS[1, 1], (0, 3), POS[1, 2], 9, 1).start()

    def k_done(m):
        k_took(m, POS[0, 2], half=0)
        k_took(m, POS[0, 2], sem=8, half=1)
        k_took(m, POS[1, 2], half=0)
        k_took(m, POS[1, 2], sem=9, half=1)

    def modulate(f):
        step = key_steps[0] if f == 0 else inf_steps[0, f - 1]
        gain = 1.0 + scale[pl.ds(step, 1), :]
        move = shift[pl.ds(step, 1), :]

        @pl.loop(0, TOK, step=64)
        def _(r):
            rows = pl.ds(r, 64)
            x = (key_lat[0, rows, :] if f == 0 else inf_lat[0, f - 1, rows, :]).astype(jnp.float32)
            x = x - jnp.mean(x, axis=-1, keepdims=True)
            x = x * lax.rsqrt(jnp.mean(x * x, axis=-1, keepdims=True) + EPSILON)
            G[f, 0, rows, :] = (x * gain + move).astype(jnp.bfloat16)

    qg = qgain[...].reshape(1, HEAD) * QSCALE
    kg = kgain[...].reshape(1, HEAD)

    def project(f, lo, hi):
        step = 4 if (hi - lo) % 4 == 0 else hi - lo
        size = step * TOK

        @pl.loop(0, (hi - lo) // step)
        def _(i):
            x = G[f, pl.ds(lo + step * i, step)].reshape(size, D)
            r = jnp.dot(x, W[...], preferred_element_type=jnp.float32)
            rows = pl.ds(pl.multiple_of(lo * TOK + i * size, 2 * TOK), size)

            def norm(t, gain):
                return (t * lax.rsqrt(jnp.mean(t * t, axis=-1, keepdims=True) + EPSILON) * gain).astype(jnp.bfloat16)

            Q[f, rows, :] = norm(r[:, :HEAD], qg)
            kv = jnp.concatenate([norm(r[:, HEAD : 2 * HEAD], kg), r[:, 2 * HEAD :].astype(jnp.bfloat16)], axis=1)
            if f == 0:
                part, base = part_of(lo)
                part[0, pl.ds(pl.multiple_of((lo - base) * TOK + i * size, 2 * TOK), size), :] = kv
            else:
                KO[f - 1, rows, :] = kv

    ones = jnp.ones((KB, HEAD), jnp.bfloat16)

    def a_copy(f, r):
        o = OFFSETS[r // 2]
        back = (r % 2) * (SLOTS // 2) + POS[o[0], (4 - o[1]) % 4]
        return pltpu.make_async_remote_copy(
            src_ref=ATT.at[f, r], dst_ref=AR.at[f, :, pl.ds(back * HEAD, HEAD)], send_sem=a_send.at[f],
            recv_sem=a_recv.at[f], device_id=at_seq(*o, r % 2), device_id_type=MESH,
        )

    def attend(f, lo, hi, sources, first, last, between):
        @pl.loop(lo, hi)
        def _(i):
            rows = pl.ds(pl.multiple_of(i * QB, QB), QB)
            q = Q[f, rows, :]
            a = None if first else ACC[f - 1, rows, :]
            for load in sources:
                kv = load()
                s = lax.dot_general(q, kv[:, :HEAD], (((1,), (1,)), ((), ())), preferred_element_type=jnp.float32)
                p = jnp.exp2(s).astype(jnp.bfloat16)
                v = jnp.concatenate([kv[:, HEAD:], ones], axis=1)
                t = jnp.dot(p, v, preferred_element_type=jnp.float32)
                a = t if a is None else a + t
            if not last:
                ACC[f - 1, rows, :] = a
            else:
                o = (a[:, :HEAD] / a[:, HEAD:]).astype(jnp.bfloat16)
                per = QB // TOK
                ATT[f, pl.ds(i * per, per)] = o.reshape(per, TOK, HEAD)
                for n in range(lo, hi):

                    @pl.when(i == n)
                    def _(n=n):
                        for r in range(n * per, (n + 1) * per):
                            if r == 0:
                                AR[f, :, 0:HEAD] = o[:TOK]
                            else:
                                a_copy(f, r).start()

            for n, then in between.items():
                pl.when(i == n)(then)

    def own(f, part=0):
        if f == 0:
            return [
                lambda n=n, j=j: KV[n][0, j * KB : (j + 1) * KB, :]
                for n, (lo, hi) in enumerate(PARTS)
                for j in range((hi - lo) * TOK // KB)
            ]
        half = SLOTS * TOK // KB // 2
        return [
            lambda j=j: KO[f - 1, j * KB : (j + 1) * KB, :] for j in range(half * part, half * (part + 1))
        ]

    def slot_of(k):
        kx, kz = k // 4, k % 4
        dx = jnp.where(kx == xh, 0, 1)
        dz = (kz - z + 4) % 4
        slot = jnp.int32(0)
        for o, i in POS.items():
            slot = jnp.where((dx == o[0]) & (dz == o[1]), i, slot)
        return slot

    ends = [slot_of(bounds[0, 0]), slot_of(bounds[0, 1])]

    def cond(*parts):
        return [
            lambda n=n, t=t, j=j: KV[n][t, j * KB : (j + 1) * KB, :]
            for n in parts
            for j in range((PARTS[n][1] - PARTS[n][0]) * TOK // KB)
            for t in ends
        ]

    def finish():
        x = AR[...].reshape(3 * TOK, SLOTS * HEAD)

        @pl.loop(0, D // 768)
        def _(n):
            cols = pl.ds(pl.multiple_of(n * 768, 256), 768)
            w = WG[:, :, :, cols].reshape(SLOTS * TOK, 768)
            t = jnp.dot(x, w, preferred_element_type=jnp.float32)
            for f in range(3):
                s = key_steps[0] if f == 0 else inf_steps[0, f - 1]
                g = gate[pl.ds(s, 1), cols]
                lat = (key_lat[0, :, cols] if f == 0 else inf_lat[0, f - 1, :, cols]).astype(jnp.float32)
                o = (lat + g * t[f * TOK : (f + 1) * TOK]).astype(jnp.bfloat16)
                if f == 0:
                    key_out[0, :, cols] = o
                else:
                    inf_out[0, f - 1, :, cols] = o

    waited, begun = set(), {}

    def need(*which):
        for n in which:
            if n not in waited:
                waited.add(n)
                loads[n].wait()

    def do_modulate(f):
        if f:
            need(3)
        modulate(f)
        if f == 0:
            pl.semaphore_wait(barrier, len(peers))

    def do_project(f, n):
        need(0, 1, 2)
        lo, hi = (CHUNKS if f == 0 else HALVES)[n]
        g_sib(f, lo, hi)
        project(f, lo, hi)

    def do_attend(f, what, lo, hi, between):
        first = (f, lo) not in begun
        parts = {"o": (own, f), "a": (own, f, 0), "b": (own, f, 1), "0": (cond, 0), "1": (cond, 1), "2": (cond, 2)}[what]
        for i in range(lo, hi):
            begun[f, i] = begun.get((f, i), 0) + 1
        attend(f, lo, hi, parts[0](*parts[1:]), first, f == 0 or begun[f, lo] == 5, between)

    simple = dict(
        gs=g_send_sib, gy=g_send_y, gx=g_send_x, fya=g_fwd_y, fyb=g_fwd_y2, fx=g_fwd_x, f2=g_fwd_2, f3a=g_fwd_3,
        f3b=g_fwd_32, f4=g_fwd_4, ks=k_send_0, k1a=k_fwd_1a, k1b=k_fwd_1b, k1c=k_fwd_1c, k2a=k_fwd_2a, k2b=k_fwd_2b,
        kd=k_done, M=do_modulate,
    )
    whole_w = dict(w0=w_0, w1a=w_1, w1b=w_1b, w1c=w_1c, w2=w_2, w3=w_3, w4a=w_4, w4b=w_4b, w5=w_5, wd=w_done)

    def run(op, between=()):
        if op in whole_w:
            whole_w[op]()
        elif op[0] == "P":
            do_project(int(op[1]), int(op[2]))
        elif op[0] == "A":
            steps = {n: [b[2:] for b in between if int(b[0]) == n] for n in {int(b[0]) for b in between}}
            thens = {n: lambda ops=ops: [run(o) for o in ops] and None for n, ops in steps.items()}
            do_attend(int(op[1]), op[2], int(op[3]), int(op[4]), thens)
        else:
            simple[op[:-1]](int(op[-1]))

    todo = [op for line in SCHEDULE for op in line.split()]
    while todo:
        op, inside = todo.pop(0), []
        while todo and todo[0][1] == "@":
            inside.append(todo.pop(0))
        run(op, inside)
    need(5)
    for f in range(3):
        whole = AR.at[f, :, pl.ds(HEAD, (SLOTS - 1) * HEAD)]
        pltpu.make_async_remote_copy(
            src_ref=whole, dst_ref=whole, send_sem=a_send.at[f], recv_sem=a_recv.at[f],
            device_id=at_seq(0, 1, 0), device_id_type=MESH,
        ).wait_recv()
    finish()

    for f in range(3):
        sent = G.at[f, pl.ds(0, 15)]
        pltpu.make_async_remote_copy(
            src_ref=sent, dst_ref=sent, send_sem=g_send.at[f], recv_sem=g_recv.at[f, 0],
            device_id=at_seq(0, 1, 0), device_id_type=MESH,
        ).wait_send()
    sent = G.at[0, pl.ds(0, 15)]
    w_copy(sent, sent, 0, at_seq(0, 1, 0)).wait_send()
    for m, (lo, hi) in enumerate(CHUNKS):
        part, base = part_of(lo)
        sent = part.at[pl.ds(0, 7), pl.ds((lo - base) * TOK, (hi - lo) * TOK)]
        pltpu.make_async_remote_copy(
            src_ref=sent, dst_ref=sent, send_sem=k_send.at[m], recv_sem=k_recv.at[m, 0],
            device_id=at_seg(0, 1), device_id_type=MESH,
        ).wait_send()
    for f in range(3):
        sent = ATT.at[f, pl.ds(1, 15)]
        pltpu.make_async_remote_copy(
            src_ref=sent, dst_ref=sent, send_sem=a_send.at[f], recv_sem=a_recv.at[f],
            device_id=at_seq(0, 1, 0), device_id_type=MESH,
        ).wait_send()


def local(
    keyframe_latents, keyframe_steps, infill_latents, infill_steps, bounds, shift_table, scale_table, gate_table,
    query_weight, key_weight, value_weight, out_weight, query_gain, key_gain,
):
    vmem, smem = pl.BlockSpec(memory_space=pltpu.VMEM), pl.BlockSpec(memory_space=pltpu.SMEM)
    hbm = pl.BlockSpec(memory_space=pl.ANY)
    bf16, f32 = jnp.bfloat16, jnp.float32
    n_tok = SLOTS * TOK
    return pl.pallas_call(
        kernel,
        name="diffusion_block",
        out_shape=(
            jax.ShapeDtypeStruct(keyframe_latents.shape, bf16),
            jax.ShapeDtypeStruct(infill_latents.shape, bf16),
        ),
        in_specs=[vmem, hbm, smem, smem, smem, vmem, vmem, hbm, hbm, hbm, hbm, hbm, vmem, vmem],
        out_specs=(vmem, vmem),
        scratch_shapes=[
            pltpu.VMEM((3, SLOTS, TOK, D), bf16),
            pltpu.VMEM((2, SLOTS // 2, TOK, D), bf16),
            *[pltpu.VMEM((8, (hi - lo) * TOK, 2 * HEAD), bf16) for lo, hi in PARTS],
            pltpu.VMEM((2, n_tok, 2 * HEAD), bf16),
            pltpu.VMEM((3, n_tok, HEAD), bf16),
            pltpu.VMEM((2, n_tok, 2 * HEAD), f32),
            pltpu.VMEM((3, SLOTS, TOK, HEAD), bf16),
            pltpu.VMEM((3, TOK, SLOTS * HEAD), bf16),
            pltpu.VMEM((D, 3 * HEAD), bf16),
            pltpu.VMEM(infill_latents.shape, bf16),
            pltpu.VMEM(gate_table.shape, f32),
            pltpu.SemaphoreType.DMA((3,)),
            pltpu.SemaphoreType.DMA((3, 18)),
            pltpu.SemaphoreType.DMA,
            pltpu.SemaphoreType.DMA((17,)),
            pltpu.SemaphoreType.DMA((4,)),
            pltpu.SemaphoreType.DMA((4, 10)),
            pltpu.SemaphoreType.DMA((3,)),
            pltpu.SemaphoreType.DMA((3,)),
            pltpu.SemaphoreType.DMA((6,)),
        ],
        compiler_params=pltpu.CompilerParams(
            collective_id=0, has_side_effects=True, vmem_limit_bytes=62 * 2**20
        ),
    )(
        keyframe_latents, infill_latents, keyframe_steps, infill_steps, bounds, shift_table, scale_table, gate_table,
        query_weight, key_weight, value_weight, out_weight, query_gain, key_gain,
    )


def solution(mesh):
    return jax.shard_map(
        local,
        mesh=mesh,
        in_specs=(
            P("seg", "seq", None), P("seg"), P("seg", None, "seq", None), P("seg", None), P("seg", None),
            P(), P(), P(), P(None, "seq"), P(None, "seq"), P(None, "seq"), P("seq", None), P(), P(),
        ),
        out_specs=(P("seg", "seq", None), P("seg", None, "seq", None)),
        check_vma=False,
    )
```
